512 devices in a mesh: space: 64 (over z, y_hi, x), summ: 8 (over y_lo, core).
Axes of the slice: x: 4, y: 8 (y_hi: 2, y_lo: 4; y = y_hi * 4 + y_lo), z: 8, core: 2. Of those that a mesh axis runs over, the one named last changes fastest.
Arguments:
- tokens: bfloat16 [64, 8, 32, 1024], P('space', None, None, 'summ'), may hold values from -8 to 8
- tile_map: int32 [64], replicated, may hold values from 0 to 63, each once
- norm_gain: float32 [1024], replicated, may hold values from 0.5 to 1.5
- q_weight: bfloat16 [1024, 1024], P(None, 'summ'), may hold values from -1.5 to 1.5
- k_weight: bfloat16 [1024, 1024], P(None, 'summ'), may hold values from -1.5 to 1.5
- v_weight: bfloat16 [1024, 1024], P(None, 'summ'), may hold values from -0.1875 to 0.1875
- out_weight: bfloat16 [1024, 1024], P('summ'), may hold values from -0.1875 to 0.1875
- pos_bias: float32 [16, 7, 7], P('summ'), may hold values from 1 to 4
- sum_keys: bfloat16 [4096, 1024], P('summ'), may hold values from -64 to 64
- sum_values: bfloat16 [4096, 1024], P('summ'), may hold values from -6 to 6
Outputs:
- mixed: bfloat16 [64, 8, 32, 1024], P('space', None, None, 'summ')
The draws below stay inside these ranges and needn't reach their ends.
Inputs may be any that keep to these rules, and one draw needn't show every extreme that they name: Block b of tokens holds the grid tile tile_map[b], counted row by row with 8 tiles a row; every tile is held once.
All inputs are finite; a program needn't handle non-finite values.
Results may differ from the reference program's by a relative error of at most 0.02.
Values may be sent and summed in bfloat16 or wider, within the bound.
A program may use at most 128 MiB of HBM per device.

```python
import math
import jax
import jax.numpy as jnp
from jax import lax

D = 1024
HEADS = 16
HD = 64
SUMMARY = 4096
HALO = 3
TX = 8
BW = 32
BH = 8
TY = 8
N_SPACE = 64


def clipped_normal(key, salt, shape):
    return jnp.clip(jax.random.normal(jax.random.fold_in(key, salt), shape, jnp.float32), -6.0, 6.0)


def draw_q_weight(key, part):
    result = clipped_normal(key, 33, (D, D)) * D ** (-0.5)
    return jnp.clip(result, -1.5, 1.5).astype(jnp.bfloat16)


def draw_k_weight(key, part):
    result = clipped_normal(key, 35, (D, D)) * D ** (-0.5)
    return jnp.clip(result, -1.5, 1.5).astype(jnp.bfloat16)


def draw_tokens(key, part):
    shape = (N_SPACE, BH, BW, D)
    base = clipped_normal(key, 41, shape)
    result = base
    return result.astype(jnp.bfloat16)


def draw_sum_keys(key, part):
    base = clipped_normal(key, 51, (SUMMARY, D))
    result = base
    return result.astype(jnp.bfloat16)


def block_scale(own_key, extent, pieces, low, largest):
    def one(axis_at, blocks):
        draws = jax.random.uniform(jax.random.fold_in(jax.random.fold_in(own_key, 6), axis_at), (blocks,), jnp.float32, low / len(pieces), largest / len(pieces))
        return jnp.repeat(jnp.exp(draws), extent[axis_at] // blocks).reshape((-1,) + (1,) * (len(extent) - axis_at - 1))

    factor_of = one(*pieces[0])
    for cut in pieces[1:]:
        factor_of = factor_of * one(*cut)
    return factor_of


def gaussian(rng, extent, deviation, reach, pieces=(), kind=jnp.bfloat16):
    values = jax.random.normal(rng, extent, jnp.float32) * deviation
    if len(pieces) > 0:
        values = block_scale(rng, extent, pieces, -0.22, 0.18) * values
    return jnp.clip(values, min=-reach, max=reach).astype(kind)


def setup_inputs(seed: int = 0) -> dict:
    keys = jax.random.split(jax.random.key(seed), 11)
    tokens = draw_tokens(jax.random.fold_in(keys[10], 71), 0)
    tile_map = jax.random.permutation(keys[1], N_SPACE).astype(jnp.int32)
    norm_gain = jnp.clip(1.0 + 0.1 * jax.random.normal(keys[2], (D,), jnp.float32), 0.5, 1.5)
    q_weight = draw_q_weight(jax.random.fold_in(keys[10], 71), 0)
    k_weight = draw_k_weight(jax.random.fold_in(keys[10], 71), 0)
    v_weight = gaussian(keys[5], (D, D), D ** -0.5, 0.1875, ((1, 8),))
    out_weight = gaussian(keys[6], (D, D), D ** -0.5, 0.1875, ((0, 8),))
    pos_bias = jnp.clip(1.0 + 3.0 * jax.random.uniform(keys[7], (HEADS, 2 * HALO + 1, 2 * HALO + 1), jnp.float32) ** block_scale(keys[7], (HEADS, 2 * HALO + 1, 2 * HALO + 1), ((0, 8),), -0.2, 0.2), 1.0, 4.0)
    sum_keys = draw_sum_keys(jax.random.fold_in(keys[10], 71), 0)
    sum_values = gaussian(keys[9], (SUMMARY, D), 1.0, 6.0, ((0, 8),))
    return {"tokens": tokens, "tile_map": tile_map, "norm_gain": norm_gain, "q_weight": q_weight, "k_weight": k_weight, "v_weight": v_weight, "out_weight": out_weight, "pos_bias": pos_bias, "sum_keys": sum_keys, "sum_values": sum_values}


EPSILON = 1e-05

def normalize(raw_values, norm_gain):
    floats = raw_values.astype(jnp.float32)
    mean_square = lax.optimization_barrier(jnp.mean(floats * floats, axis=-1, keepdims=True))
    return (floats * lax.rsqrt(mean_square + EPSILON) * norm_gain).astype(jnp.bfloat16)

def summary_part(query_rows, key_rows, value_rows):
    scores = jnp.dot(query_rows, key_rows.T, preferred_element_type=jnp.float32) * HD ** (-0.5)
    row_max = lax.optimization_barrier(jnp.max(scores, axis=-1))
    weights = jnp.exp(scores - row_max[:, None])
    weight_sum = lax.optimization_barrier(jnp.sum(weights, axis=-1))
    weighted = jnp.dot(weights.astype(jnp.bfloat16), value_rows, preferred_element_type=jnp.float32)
    return (row_max, weight_sum, weighted)

def reference(tokens, tile_map, norm_gain, q_weight, k_weight, v_weight, out_weight, pos_bias, sum_keys, sum_values):
    head_count = D // HD
    grid_rows = TY * BH
    grid_cols = TX * BW
    token_total = grid_rows * grid_cols
    score_scale = HD ** (-0.5)
    placed = jnp.zeros_like(tokens).at[tile_map].set(tokens)
    token_grid = placed.reshape(TY, TX, BH, BW, D).transpose(0, 2, 1, 3, 4).reshape(token_total, D)
    normed = normalize(token_grid, norm_gain)
    queries = jnp.dot(normed, q_weight, preferred_element_type=jnp.float32).astype(jnp.bfloat16)
    keys_all = jnp.dot(normed, k_weight, preferred_element_type=jnp.float32).astype(jnp.bfloat16)
    values_all = jnp.dot(normed, v_weight, preferred_element_type=jnp.float32).astype(jnp.bfloat16)
    query_grid = queries.reshape(grid_rows, grid_cols, head_count, HD).astype(jnp.float32)
    pad_spec = ((HALO, HALO), (HALO, HALO), (0, 0), (0, 0))
    key_pad = jnp.pad(keys_all.reshape(grid_rows, grid_cols, head_count, HD), pad_spec)
    value_pad = jnp.pad(values_all.reshape(grid_rows, grid_cols, head_count, HD), pad_spec)
    inside = jnp.pad(jnp.ones((grid_rows, grid_cols), dtype=bool), HALO)
    window_span = 2 * HALO + 1
    score_list = []
    for row_off in range(window_span):
        for col_off in range(window_span):
            shifted = key_pad[row_off:row_off + grid_rows, col_off:col_off + grid_cols].astype(jnp.float32)
            window_score = lax.optimization_barrier(jnp.sum(query_grid * shifted, axis=-1)) * score_scale + pos_bias[:, row_off, col_off]
            visible = inside[row_off:row_off + grid_rows, col_off:col_off + grid_cols][..., None]
            score_list.append(jnp.where(visible, window_score, -jnp.inf))
    window_scores = jnp.stack(score_list)
    window_max = lax.optimization_barrier(jnp.max(window_scores, axis=0))
    window_weights = jnp.exp(window_scores - window_max[None])
    window_sum = lax.optimization_barrier(jnp.sum(window_weights, axis=0))
    window_weighted = jnp.zeros((grid_rows, grid_cols, head_count, HD), jnp.float32)
    offset_index = 0
    for row_off in range(window_span):
        for col_off in range(window_span):
            shifted = value_pad[row_off:row_off + grid_rows, col_off:col_off + grid_cols].astype(jnp.float32)
            factor = window_weights[offset_index].astype(jnp.bfloat16).astype(jnp.float32)
            window_weighted = window_weighted + factor[..., None] * shifted
            offset_index += 1
    block_rows = math.gcd(token_total, 4096)
    query_heads = queries.reshape(token_total, head_count, HD).transpose(1, 0, 2)
    query_heads = query_heads.reshape(head_count, token_total // block_rows, block_rows, HD)
    key_heads = sum_keys.reshape(SUMMARY, head_count, HD).transpose(1, 0, 2)
    value_heads = sum_values.reshape(SUMMARY, head_count, HD).transpose(1, 0, 2)

    def per_head(operands):
        query_blocks, key_rows, value_rows = operands
        return lax.map(lambda query_block: summary_part(query_block, key_rows, value_rows), query_blocks)
    global_max, global_sum, global_weighted = lax.map(per_head, (query_heads, key_heads, value_heads))
    global_max = global_max.reshape(head_count, token_total).T
    global_sum = global_sum.reshape(head_count, token_total).T
    global_weighted = global_weighted.reshape(head_count, token_total, HD).transpose(1, 0, 2)
    window_max = window_max.reshape(token_total, head_count)
    window_sum = window_sum.reshape(token_total, head_count)
    window_weighted = window_weighted.reshape(token_total, head_count, HD)
    joint_max = jnp.maximum(window_max, global_max)
    window_factor = jnp.exp(window_max - joint_max)
    global_factor = jnp.exp(global_max - joint_max)
    weight_sum = window_sum * window_factor + global_sum * global_factor
    weighted = window_weighted * window_factor[..., None] + global_weighted * global_factor[..., None]
    attended = (weighted / weight_sum[..., None]).reshape(token_total, D).astype(jnp.bfloat16)
    mixed_rows = jnp.dot(attended, out_weight, preferred_element_type=jnp.float32).astype(jnp.bfloat16)
    tiles_out = mixed_rows.reshape(TY, BH, TX, BW, D).transpose(0, 2, 1, 3, 4).reshape(N_SPACE, BH, BW, D)
    return tiles_out[tile_map]
```

```python
from functools import partial

import numpy as np
import jax
import jax.numpy as jnp
from jax import lax
from jax.experimental import pallas as pl
from jax.experimental.pallas import tpu as pltpu
from jax.sharding import PartitionSpec as P

D = 1024
HD = 64
HALO = 3
TX = 8
BW = 32
BH = 8
EPSILON = 1e-05
WIN = 2 * HALO + 1
TOK = BH * BW
LANES = 128
X = 4
YH = 2
YL = 4
CORES = 2
HIDDEN = -1e30
UNIT = 16
UNIT_STEP = (
    [(-1, 0)] * 6
    + [(1, 0)] * 6
    + [(0, -1)] * 2
    + [(0, 1)] * 2
    + [(-1, -1), (-1, 1), (1, -1), (1, 1)]
)
N_UNIT = len(UNIT_STEP)
HALO_KEYS = N_UNIT * UNIT
BAND = HALO * BW
SIDE_ROWS = HALO_KEYS - 2 * BAND
ROUTER_STRIDE = 3
MESH = pl.DeviceIdType.MESH


def halo_positions():
    places = [(-HALO + j // BW, j % BW, (BH - HALO) * BW + j) for j in range(BAND)]
    places += [(BH + j // BW, j % BW, j) for j in range(BAND)]

    def side(count, rows, padded, row_at, col_at, from_row, from_col):
        out = []
        for i in range(padded):
            r, c = i // HALO, i % HALO
            out.append((row_at + r, col_at + c, (from_row + r) * BW + from_col + c) if i < count else None)
        return out

    places += side(BH * HALO, BH, 2 * UNIT, 0, -HALO, 0, BW - HALO)
    places += side(BH * HALO, BH, 2 * UNIT, 0, BW, 0, 0)
    places += side(HALO * HALO, HALO, UNIT, -HALO, -HALO, BH - HALO, BW - HALO)
    places += side(HALO * HALO, HALO, UNIT, -HALO, BW, BH - HALO, 0)
    places += side(HALO * HALO, HALO, UNIT, BH, -HALO, 0, BW - HALO)
    places += side(HALO * HALO, HALO, UNIT, BH, BW, 0, 0)
    return places


def offset_codes():
    keys = [(k // BW, k % BW) for k in range(TOK)]
    keys += [(None if place is None else place[:2]) for place in halo_positions()]
    codes = np.full((len(keys), TOK), -1, np.int32)
    rows, cols = np.arange(TOK) // BW, np.arange(TOK) % BW
    for at, key in enumerate(keys):
        if key is None:
            continue
        i, j = key[0] - rows + HALO, key[1] - cols + HALO
        near = (i >= 0) & (i < WIN) & (j >= 0) & (j < WIN)
        codes[at] = np.where(near, i * WIN + j, -1)
    return codes


def side_picks():
    picks = np.zeros((SIDE_ROWS, TOK), np.float32)
    for at, place in enumerate(halo_positions()[2 * BAND :]):
        if place is not None:
            picks[at, place[2]] = 1.0
    return picks


def kernel(
    n_space,
    tile_map,
    pos_bias,
    tokens,
    gain,
    q_weight,
    k_weight,
    v_weight,
    out_weight,
    sum_keys,
    sum_values,
    codes_in,
    picks_in,
    out,
    gathered,
    normed,
    weights,
    out_w,
    codes,
    picks,
    bias,
    own_k,
    keys,
    values,
    values_t,
    queries,
    part_out,
    part_in,
    stat_out,
    stat_in,
    inverse,
    inverse_s,
    pack,
    routed,
    staged,
    halo,
    terms,
    pair_in,
    pair_sum,
    line_in,
    load_sem,
    inverse_sem,
    tok_send,
    tok_recv,
    k_send,
    k_recv,
    v_send,
    v_recv,
    q_send,
    q_recv,
    part_send,
    part_recv,
    stat_send,
    stat_recv,
    rim_send,
    rim_recv,
    halo_send,
    halo_recv,
    pair_send,
    pair_recv,
    line_send,
    line_recv,
):
    slots = routed.shape[0]
    share = keys.shape[1]
    ty = n_space // TX
    me = lax.axis_index("space")
    my_summ = lax.axis_index("summ")
    y_lo, core = my_summ // CORES, my_summ % CORES
    x_at = me % X
    y_hi = (me // X) % YH
    z_at = me // (X * YH)
    y_at = y_hi * YL + y_lo
    sibling = y_lo * CORES + 1 - core

    def local(src, dst, sem):
        return pltpu.make_async_copy(src, dst, sem)

    def remote(src, dst, send, recv, space, summ):
        return pltpu.make_async_remote_copy(
            src_ref=src,
            dst_ref=dst,
            send_sem=send,
            recv_sem=recv,
            device_id=(space, summ),
            device_id_type=MESH,
        )

    def ring(step, to_core):
        y = (y_at + step + YH * YL) % (YH * YL)
        return (z_at * YH + y // YL) * X + x_at, (y % YL) * CORES + to_core

    def line(step):
        return (y_lo + step) % YL

    loads = [
        local(q_weight, weights.at[:, 0:LANES], load_sem.at[0]),
        local(k_weight, weights.at[:, LANES : 2 * LANES], load_sem.at[1]),
        local(v_weight, weights.at[:, 2 * LANES : 3 * LANES], load_sem.at[2]),
        local(out_weight, out_w, load_sem.at[3]),
        local(codes_in, codes, load_sem.at[4]),
        local(picks_in, picks, load_sem.at[5]),
    ]
    own_tokens = local(tokens, gathered.at[my_summ], tok_recv.at[my_summ])
    own_tokens.start()
    my_rows = pl.ds(pl.multiple_of(x_at * share, share), share)
    my_cols = pl.ds(pl.multiple_of(my_summ * LANES, LANES), LANES)
    local(sum_keys.at[my_rows, my_cols], keys.at[my_summ], k_recv).start()
    local(sum_values.at[my_rows, my_cols], values.at[my_summ], v_recv).start()

    barrier = pltpu.get_barrier_semaphore()

    def greet(space, summ):
        pl.semaphore_signal(barrier, inc=1, device_id=(space, summ), device_id_type=MESH)

    greet(me, sibling)
    for step in range(1, YL):
        greet(me, line(step) * CORES + core)
    for step in (1, -1, 2, -2):
        for to_core in range(CORES):
            greet(*ring(step, to_core))

    def greet_space(step, carry):
        greet((me + step) % n_space, my_summ)
        return carry

    lax.fori_loop(1, n_space, greet_space, 0)
    for load in loads:
        load.start()
    pl.semaphore_wait(barrier, 1 + (YL - 1) + 4 * CORES + n_space - 1)

    sends = []
    for at, step in enumerate((2, 1, 3)):
        sends.append(
            remote(
                tokens,
                gathered.at[my_summ],
                tok_send.at[at],
                tok_recv.at[my_summ],
                me,
                line(step) * CORES + core,
            )
        )
    sends.append(
        remote(tokens, gathered.at[my_summ], tok_send.at[3], tok_recv.at[my_summ], me, sibling)
    )
    for send in sends:
        send.start()

    def give(source, held, send_sem, recv_sem, space, summ):
        cols = pl.ds(pl.multiple_of(summ * LANES, LANES), LANES)
        remote(source.at[my_rows, cols], held.at[my_summ], send_sem, recv_sem, space, summ).start()

    def give_summary():
        for step in (1, -1):
            for to_core in range(CORES):
                give(sum_keys, keys, k_send, k_recv, *ring(step, to_core))
        for to_core in range(CORES):
            give(sum_keys, keys, k_send, k_recv, *ring(2, to_core))
        give(sum_keys, keys, k_send, k_recv, me, sibling)
        for step in (1, -1):
            for to_core in range(CORES):
                give(sum_values, values, v_send, v_recv, *ring(step, to_core))
        for to_core in range(CORES):
            give(sum_values, values, v_send, v_recv, *ring(-2, to_core))
        give(sum_values, values, v_send, v_recv, me, sibling)

    lane = lax.broadcasted_iota(jnp.int32, inverse.shape, 1)

    def place(at, so_far):
        return so_far + jnp.where(lane == tile_map[at], at, 0)

    inverse[...] = lax.fori_loop(0, n_space, place, jnp.zeros(inverse.shape, jnp.int32))
    to_scalars = local(inverse, inverse_s, inverse_sem)
    to_scalars.start()

    loads[4].wait()

    def fill(at, carry):
        rows = pl.ds(pl.multiple_of(at * UNIT, UNIT), UNIT)
        code = codes[rows, :]
        first = jnp.full(code.shape, HIDDEN, jnp.float32)
        second = first
        for i in range(WIN):
            for j in range(WIN):
                here = code == i * WIN + j
                first = jnp.where(here, pos_bias[0, i, j], first)
                second = jnp.where(here, pos_bias[1, i, j], second)
        bias[0, rows, :] = first
        bias[1, rows, :] = second
        return carry

    lax.fori_loop(0, bias.shape[1] // UNIT, fill, 0)
    my_tile = tile_map[me]
    tile_row, tile_col = my_tile // TX, my_tile % TX
    edge = {
        (-1, 0): jnp.where(tile_row > 0, 0.0, HIDDEN),
        (1, 0): jnp.where(tile_row < ty - 1, 0.0, HIDDEN),
        (0, -1): jnp.where(tile_col > 0, 0.0, HIDDEN),
        (0, 1): jnp.where(tile_col < TX - 1, 0.0, HIDDEN),
    }
    for down in (-1, 1):
        for across in (-1, 1):
            edge[down, across] = jnp.minimum(edge[down, 0], edge[0, across])
    for step, hidden in edge.items():
        at = TOK + UNIT_STEP.index(step) * UNIT
        rows = slice(at, at + UNIT_STEP.count(step) * UNIT)
        for h in range(2):
            bias[h, rows, :] = bias[h, rows, :] + hidden

    forwards = []
    for at, step in enumerate((1, 3, 2)):
        slab = line(step) * CORES + core
        local(gathered.at[slab], gathered.at[slab], tok_recv.at[slab]).wait()
        forward = remote(
            gathered.at[slab],
            gathered.at[slab],
            tok_send.at[4 + at],
            tok_recv.at[slab],
            me,
            sibling,
        )
        forward.start()
        forwards.append(forward)
    own_tokens.wait()
    for step in range(YL):
        slab = line(step) * CORES + 1 - core
        local(gathered.at[slab], gathered.at[slab], tok_recv.at[slab]).wait()
    give_summary()

    squares = jnp.zeros((TOK, LANES), jnp.float32)
    for slab in range(YL * CORES):
        floats = gathered[slab].astype(jnp.float32)
        squares = squares + floats * floats
    scale = lax.rsqrt(jnp.sum(squares, axis=-1, keepdims=True) * (1.0 / D) + EPSILON)
    for slab in range(YL * CORES):
        cols = slice(slab * LANES, (slab + 1) * LANES)
        floats = gathered[slab].astype(jnp.float32)
        normed[:, cols] = (floats * scale * gain[:, cols]).astype(jnp.bfloat16)
    for load in loads[:3]:
        load.wait()
    projected = jnp.dot(normed[...], weights[...], preferred_element_type=jnp.float32)
    projected = projected.astype(jnp.bfloat16)
    own_k[...] = projected[:, LANES : 2 * LANES]
    own_v = projected[:, 2 * LANES :]

    loads[5].wait()
    sides = jnp.dot(picks[...], projected[:, LANES:], preferred_element_type=jnp.float32)
    sides = sides.astype(jnp.bfloat16)
    for which in range(2):
        own = projected[:, (1 + which) * LANES : (2 + which) * LANES]
        first = which * N_UNIT
        bands = BAND // UNIT
        pack[first : first + bands] = own[TOK - BAND :].reshape(bands, UNIT, LANES)
        pack[first + bands : first + 2 * bands] = own[:BAND].reshape(bands, UNIT, LANES)
        pack[first + 2 * bands : first + N_UNIT] = sides[
            :, which * LANES : (which + 1) * LANES
        ].reshape(N_UNIT - 2 * bands, UNIT, LANES)

    def send_rim(unit, carry):
        router = (unit * ROUTER_STRIDE) % n_space
        slot = unit // n_space

        @pl.when(router != me)
        def _():
            remote(
                pack.at[unit],
                routed.at[slot, me],
                rim_send,
                rim_recv.at[slot],
                router,
                my_summ,
            ).start()

        @pl.when(router == me)
        def _():
            local(pack.at[unit], routed.at[slot, me], rim_recv.at[slot]).start()

        return carry

    lax.fori_loop(0, 2 * N_UNIT, send_rim, 0)

    scaled = projected[:, :LANES].astype(jnp.float32) * HD ** (-0.5)
    queries[x_at] = scaled.T.astype(jnp.bfloat16)
    peers = [(x_at + step) % X for step in range(X)]
    for step in range(1, X):
        remote(
            queries.at[x_at],
            queries.at[x_at],
            q_send,
            q_recv.at[x_at],
            me - x_at + peers[step],
            my_summ,
        ).start()

    def one_head(both, h):
        blank = jnp.zeros((HD, TOK), jnp.bfloat16)
        own = both[h * HD : (h + 1) * HD]
        return jnp.concatenate([own, blank] if h == 0 else [blank, own], axis=0)

    def attend(scores, v_rows):
        top = jnp.max(scores, axis=0, keepdims=True)
        weight = jnp.exp(scores - top)
        total = jnp.sum(weight, axis=0, keepdims=True)
        summed = jnp.dot(v_rows, weight.astype(jnp.bfloat16), preferred_element_type=jnp.float32)
        return top, total, summed

    my_queries = queries[x_at]
    own_vt = own_v.astype(jnp.float32).T.astype(jnp.bfloat16)
    parts = [[], []]
    for h in range(2):
        scores = jnp.dot(own_k[...], one_head(my_queries, h), preferred_element_type=jnp.float32)
        parts[h].append(attend(scores + bias[h, :TOK], own_vt[h * HD : (h + 1) * HD]))

    to_scalars.wait()
    first_unit = (me * pow(ROUTER_STRIDE, -1, n_space)) % n_space
    for slot in range(slots):
        unit = first_unit + slot * n_space

        @pl.when(unit < 2 * N_UNIT)
        def _():
            local(routed.at[slot], routed.at[slot], rim_recv.at[slot]).wait()
            kind = unit % N_UNIT
            down = jnp.where(
                kind < 6, -1, jnp.where(kind < 12, 1, jnp.where(kind < 16, 0, jnp.where(kind < 18, -1, 1)))
            )
            across = jnp.where(
                kind < 12,
                0,
                jnp.where(kind < 14, -1, jnp.where(kind < 16, 1, jnp.where(kind % 2 == 0, -1, 1))),
            )

            def pass_on(to, carry):
                tile = tile_map[to]
                row = jnp.clip(tile // TX + down, 0, ty - 1)
                col = jnp.clip(tile % TX + across, 0, TX - 1)
                holder = jnp.clip(inverse_s[0, row * TX + col], 0, n_space - 1)
                staged[slot, to] = routed[slot, holder]

                @pl.when(to != me)
                def _():
                    remote(
                        staged.at[slot, to], halo.at[unit], halo_send, halo_recv, to, my_summ
                    ).start()

                @pl.when(to == me)
                def _():
                    local(staged.at[slot, to], halo.at[unit], halo_recv).start()

                return carry

            lax.fori_loop(0, n_space, pass_on, 0)

    local(values, values, v_recv).wait()
    for slab in range(YL * CORES):
        values_t[:, slab * share : (slab + 1) * share] = (
            values[slab].astype(jnp.float32).T.astype(jnp.bfloat16)
        )
    local(keys, keys, k_recv).wait()

    def summary(step, carry):
        peer = (x_at + step) % X

        @pl.when(step > 0)
        def _():
            local(queries.at[peer], queries.at[peer], q_recv.at[peer]).wait()

        theirs = queries[peer]
        key_rows = keys[...].reshape(YL * CORES * share, LANES)
        tops, totals, sums = [], [], []
        for h in range(2):
            scores = jnp.dot(key_rows, one_head(theirs, h), preferred_element_type=jnp.float32)
            top, total, summed = attend(scores, values_t[h * HD : (h + 1) * HD, :])
            tops.append(top)
            totals.append(total)
            sums.append(summed)
        part_out[peer] = jnp.concatenate(sums, axis=0).astype(jnp.bfloat16)
        stat_out[peer] = jnp.concatenate(tops + totals + [jnp.zeros((4, TOK), jnp.float32)], axis=0)

        @pl.when(step > 0)
        def _():
            to = me - x_at + peer
            remote(
                part_out.at[peer], part_in.at[x_at], part_send, part_recv.at[x_at], to, my_summ
            ).start()
            remote(
                stat_out.at[peer], stat_in.at[x_at], stat_send, stat_recv.at[x_at], to, my_summ
            ).start()

        return carry

    lax.fori_loop(0, X, summary, 0)

    local(halo, halo, halo_recv).wait()
    halo_k = halo[:N_UNIT].reshape(HALO_KEYS, LANES)
    halo_vt = halo[N_UNIT:].reshape(HALO_KEYS, LANES).astype(jnp.float32).T.astype(jnp.bfloat16)
    for h in range(2):
        scores = jnp.dot(halo_k, one_head(my_queries, h), preferred_element_type=jnp.float32)
        parts[h].append(attend(scores + bias[h, TOK:], halo_vt[h * HD : (h + 1) * HD]))

    for step in range(X):
        peer = peers[step]
        if step > 0:
            local(part_in.at[peer], part_in.at[peer], part_recv.at[peer]).wait()
            local(stat_in.at[peer], stat_in.at[peer], stat_recv.at[peer]).wait()
            rows, stats = part_in[peer], stat_in[peer]
        else:
            rows, stats = part_out[peer], stat_out[peer]
        for h in range(2):
            parts[h].append(
                (
                    stats[h : h + 1],
                    stats[2 + h : 3 + h],
                    rows[h * HD : (h + 1) * HD].astype(jnp.float32),
                )
            )
    heads = []
    for h in range(2):
        joint = parts[h][0][0]
        for top, _, _ in parts[h][1:]:
            joint = jnp.maximum(joint, top)
        total = jnp.zeros((1, TOK), jnp.float32)
        summed = jnp.zeros((HD, TOK), jnp.float32)
        for top, part_total, part_sum in parts[h]:
            factor = jnp.exp(top - joint)
            total = total + part_total * factor
            summed = summed + part_sum * factor
        heads.append(summed / total)
    attended = jnp.concatenate(heads, axis=0).T.astype(jnp.bfloat16)

    loads[3].wait()
    mixed = jnp.dot(attended, out_w[...], preferred_element_type=jnp.float32).astype(jnp.bfloat16)
    for at in range(YL):
        for side in range(CORES):
            slab = at * CORES + side
            terms[side, at] = mixed[:, slab * LANES : (slab + 1) * LANES]
    order = [line(step) for step in (2, 1, 3, 0)]
    pair = []
    for at in order:
        pair.append(
            remote(
                terms.at[1 - core, at], pair_in.at[at], pair_send.at[at], pair_recv.at[at], me, sibling
            )
        )
        pair[-1].start()
    along = []
    for at in order[:3]:
        local(pair_in.at[at], pair_in.at[at], pair_recv.at[at]).wait()
        both = terms[core, at].astype(jnp.float32) + pair_in[at].astype(jnp.float32)
        pair_sum[at] = both.astype(jnp.bfloat16)
        along.append(
            remote(
                pair_sum.at[at],
                line_in.at[y_lo],
                line_send.at[at],
                line_recv.at[y_lo],
                me,
                at * CORES + core,
            )
        )
        along[-1].start()
    local(pair_in.at[y_lo], pair_in.at[y_lo], pair_recv.at[y_lo]).wait()
    result = terms[core, y_lo].astype(jnp.float32) + pair_in[y_lo].astype(jnp.float32)
    for step in (1, 3, 2):
        at = line(step)
        local(line_in.at[at], line_in.at[at], line_recv.at[at]).wait()
        result = result + line_in[at].astype(jnp.float32)
    out[...] = result.astype(jnp.bfloat16)

    for send in sends + forwards + pair + along:
        send.wait_send()
    for sem, held in ((k_send, keys), (v_send, values)):
        sent = held.at[: YL * CORES - 1]
        local(sent, sent, sem).wait()
    for sem, held in ((q_send, queries), (part_send, part_out), (stat_send, stat_out)):
        sent = held.at[: X - 1]
        local(sent, sent, sem).wait()
    routers = [(unit * ROUTER_STRIDE) % n_space for unit in range(2 * N_UNIT)]
    own_units = jnp.where(first_unit < (2 * N_UNIT) % n_space, 1, 0) + 2 * N_UNIT // n_space
    for count in sorted({routers.count(at) for at in range(n_space)}):

        @pl.when(own_units == count)
        def _():
            sent = pack.at[: 2 * N_UNIT - count]
            local(sent, sent, rim_send).wait()

    for slot in range(slots):

        @pl.when(first_unit + slot * n_space < 2 * N_UNIT)
        def _():
            sent = staged.at[slot, : n_space - 1]
            local(sent, sent, halo_send).wait()


def shards(
    n_space,
    tokens,
    tile_map,
    norm_gain,
    q_weight,
    k_weight,
    v_weight,
    out_weight,
    pos_bias,
    sum_keys,
    sum_values,
):
    share = sum_keys.shape[0] // X
    slots = -(-2 * N_UNIT // n_space)
    bf16 = jnp.bfloat16
    f32 = jnp.float32
    dma = pltpu.SemaphoreType.DMA
    anywhere = pl.BlockSpec(memory_space=pl.ANY)
    scalars = pl.BlockSpec(memory_space=pltpu.SMEM)
    vector = pl.BlockSpec(memory_space=pltpu.VMEM)
    slab = (TOK, LANES)
    turned = (LANES, TOK)
    scratch = [
        pltpu.VMEM((YL * CORES,) + slab, bf16),
        pltpu.VMEM((TOK, D), bf16),
        pltpu.VMEM((D, 3 * LANES), bf16),
        pltpu.VMEM((LANES, D), bf16),
        pltpu.VMEM((TOK + HALO_KEYS, TOK), jnp.int32),
        pltpu.VMEM((SIDE_ROWS, TOK), bf16),
        pltpu.VMEM((2, TOK + HALO_KEYS, TOK), f32),
        pltpu.VMEM(slab, bf16),
        pltpu.VMEM((YL * CORES, share, LANES), bf16),
        pltpu.VMEM((YL * CORES, share, LANES), bf16),
        pltpu.VMEM((LANES, YL * CORES * share), bf16),
        pltpu.VMEM((X,) + turned, bf16),
        pltpu.VMEM((X,) + turned, bf16),
        pltpu.VMEM((X,) + turned, bf16),
        pltpu.VMEM((X, 8, TOK), f32),
        pltpu.VMEM((X, 8, TOK), f32),
        pltpu.VMEM((8, LANES), jnp.int32),
        pltpu.SMEM((8, LANES), jnp.int32),
        pltpu.VMEM((2 * N_UNIT, UNIT, LANES), bf16),
        pltpu.VMEM((slots, n_space, UNIT, LANES), bf16),
        pltpu.VMEM((slots, n_space, UNIT, LANES), bf16),
        pltpu.VMEM((2 * N_UNIT, UNIT, LANES), bf16),
        pltpu.VMEM((CORES, YL) + slab, bf16),
        pltpu.VMEM((YL,) + slab, bf16),
        pltpu.VMEM((YL,) + slab, bf16),
        pltpu.VMEM((YL,) + slab, bf16),
        dma((6,)),
        dma,
        dma((7,)),
        dma((YL * CORES,)),
        dma,
        dma,
        dma,
        dma,
        dma,
        dma((X,)),
        dma,
        dma((X,)),
        dma,
        dma((X,)),
        dma,
        dma((slots,)),
        dma,
        dma,
        dma((YL,)),
        dma((YL,)),
        dma((YL,)),
        dma((YL,)),
    ]
    mixed = pl.pallas_call(
        partial(kernel, n_space),
        out_shape=jax.ShapeDtypeStruct(slab, bf16),
        in_specs=[scalars, scalars, anywhere, vector] + [anywhere] * 8,
        out_specs=vector,
        scratch_shapes=scratch,
        compiler_params=pltpu.CompilerParams(
            collective_id=0, has_side_effects=True, vmem_limit_bytes=48 * 1024 * 1024
        ),
        name="tile_attention",
    )(
        tile_map,
        pos_bias,
        tokens.reshape(slab),
        norm_gain.reshape(1, D),
        q_weight,
        k_weight,
        v_weight,
        out_weight,
        sum_keys,
        sum_values,
        jnp.asarray(offset_codes()),
        jnp.asarray(side_picks(), bf16),
    )
    return mixed.reshape(1, BH, BW, LANES)


def solution(mesh):
    return jax.shard_map(
        partial(shards, mesh.shape["space"]),
        mesh=mesh,
        in_specs=(
            P("space", None, None, "summ"),
            P(),
            P(),
            P(None, "summ"),
            P(None, "summ"),
            P(None, "summ"),
            P("summ", None),
            P("summ", None, None),
            P("summ", None),
            P("summ", None),
        ),
        out_specs=P("space", None, None, "summ"),
        check_vma=False,
    )
```

```python
from functools import partial

import numpy as np
import jax
import jax.numpy as jnp
from jax import lax
from jax.experimental import pallas as pl
from jax.experimental.pallas import tpu as pltpu
from jax.sharding import PartitionSpec as P

D = 1024
HD = 64
HALO = 3
TX = 8
BW = 32
BH = 8
EPSILON = 1e-05
WIN = 2 * HALO + 1
TOK = BH * BW
LANES = 128
X = 4
YH = 2
YL = 4
CORES = 2
HIDDEN = -1e30
UNIT = 16
UNIT_STEP = (
    [(-1, 0)] * 6
    + [(1, 0)] * 6
    + [(0, -1)] * 2
    + [(0, 1)] * 2
    + [(-1, -1), (-1, 1), (1, -1), (1, 1)]
)
N_UNIT = len(UNIT_STEP)
HALO_KEYS = N_UNIT * UNIT
BAND = HALO * BW
SIDE_ROWS = HALO_KEYS - 2 * BAND
LATE_Z = 5
MESH = pl.DeviceIdType.MESH


def halo_positions():
    places = [(-HALO + j // BW, j % BW, (BH - HALO) * BW + j) for j in range(BAND)]
    places += [(BH + j // BW, j % BW, j) for j in range(BAND)]

    def side(count, rows, padded, row_at, col_at, from_row, from_col):
        out = []
        for i in range(padded):
            r, c = i // HALO, i % HALO
            out.append((row_at + r, col_at + c, (from_row + r) * BW + from_col + c) if i < count else None)
        return out

    places += side(BH * HALO, BH, 2 * UNIT, 0, -HALO, 0, BW - HALO)
    places += side(BH * HALO, BH, 2 * UNIT, 0, BW, 0, 0)
    places += side(HALO * HALO, HALO, UNIT, -HALO, -HALO, BH - HALO, BW - HALO)
    places += side(HALO * HALO, HALO, UNIT, -HALO, BW, BH - HALO, 0)
    places += side(HALO * HALO, HALO, UNIT, BH, -HALO, 0, BW - HALO)
    places += side(HALO * HALO, HALO, UNIT, BH, BW, 0, 0)
    return places


def offset_codes():
    keys = [(k // BW, k % BW) for k in range(TOK)]
    keys += [(None if place is None else place[:2]) for place in halo_positions()]
    codes = np.full((len(keys), TOK), -1, np.int32)
    rows, cols = np.arange(TOK) // BW, np.arange(TOK) % BW
    for at, key in enumerate(keys):
        if key is None:
            continue
        i, j = key[0] - rows + HALO, key[1] - cols + HALO
        near = (i >= 0) & (i < WIN) & (j >= 0) & (j < WIN)
        codes[at] = np.where(near, i * WIN + j, -1)
    return codes


def side_picks():
    picks = np.zeros((SIDE_ROWS, TOK), np.float32)
    for at, place in enumerate(halo_positions()[2 * BAND :]):
        if place is not None:
            picks[at, place[2]] = 1.0
    return picks


def kernel(
    n_space,
    tile_map,
    pos_bias,
    tokens,
    gain,
    q_weight,
    k_weight,
    v_weight,
    out_weight,
    sum_keys,
    sum_values,
    codes_in,
    picks_in,
    out,
    gathered,
    normed,
    weights,
    out_w,
    codes,
    picks,
    bias,
    own_k,
    keys,
    values,
    values_t,
    queries,
    part_out,
    part_in,
    stat_out,
    stat_in,
    inverse,
    inverse_s,
    pack,
    routed,
    staged,
    halo,
    terms,
    pair_in,
    pair_sum,
    line_in,
    load_sem,
    inverse_sem,
    tok_send,
    tok_recv,
    k_send,
    k_recv,
    v_send,
    v_recv,
    q_send,
    q_recv,
    part_send,
    part_recv,
    stat_send,
    stat_recv,
    rim_send,
    rim_recv,
    halo_send,
    halo_recv,
    pair_send,
    pair_recv,
    line_send,
    line_recv,
):
    slots = routed.shape[0]
    n_routers = min(n_space, 2 * N_UNIT)
    share = keys.shape[1]
    ty = n_space // TX
    me = lax.axis_index("space")
    my_summ = lax.axis_index("summ")
    y_lo, core = my_summ // CORES, my_summ % CORES
    x_at = me % X
    y_hi = (me // X) % YH
    z_at = me // (X * YH)
    y_at = y_hi * YL + y_lo
    sibling = y_lo * CORES + 1 - core

    def local(src, dst, sem):
        return pltpu.make_async_copy(src, dst, sem)

    def remote(src, dst, send, recv, space, summ):
        return pltpu.make_async_remote_copy(
            src_ref=src,
            dst_ref=dst,
            send_sem=send,
            recv_sem=recv,
            device_id=(space, summ),
            device_id_type=MESH,
        )

    def ring(step, to_core):
        y = (y_at + step + YH * YL) % (YH * YL)
        return (z_at * YH + y // YL) * X + x_at, (y % YL) * CORES + to_core

    def line(step):
        return (y_lo + step) % YL

    loads = [
        local(q_weight, weights.at[:, 0:LANES], load_sem.at[0]),
        local(k_weight, weights.at[:, LANES : 2 * LANES], load_sem.at[1]),
        local(v_weight, weights.at[:, 2 * LANES : 3 * LANES], load_sem.at[2]),
        local(out_weight, out_w, load_sem.at[3]),
        local(codes_in, codes, load_sem.at[4]),
        local(picks_in, picks, load_sem.at[5]),
    ]
    own_tokens = local(tokens, gathered.at[my_summ], tok_recv.at[my_summ])
    own_tokens.start()
    my_rows = pl.ds(pl.multiple_of(x_at * share, share), share)
    my_cols = pl.ds(pl.multiple_of(my_summ * LANES, LANES), LANES)
    local(sum_keys.at[my_rows, my_cols], keys.at[my_summ], k_recv).start()
    local(sum_values.at[my_rows, my_cols], values.at[my_summ], v_recv).start()

    barrier = pltpu.get_barrier_semaphore()

    def greet(space, summ):
        pl.semaphore_signal(barrier, inc=1, device_id=(space, summ), device_id_type=MESH)

    greet(me, sibling)
    for step in range(1, YL):
        greet(me, line(step) * CORES + core)
    for step in (1, -1, 2, -2):
        for to_core in range(CORES):
            greet(*ring(step, to_core))

    for step in range(1, X):
        greet(me - x_at + (x_at + step) % X, my_summ)

    def greet_space(step, carry):
        greet((me + step) % n_space, my_summ)
        return carry

    @pl.when(me < n_routers)
    def _():
        lax.fori_loop(1, n_space, greet_space, 0)

    for load in loads:
        load.start()
    near = 1 + (YL - 1) + 4 * CORES + (X - 1)
    pl.semaphore_wait(barrier, near + n_routers - jnp.where(me < n_routers, 1, 0))

    sends = []
    for at, step in enumerate((2, 1, 3)):
        sends.append(
            remote(
                tokens,
                gathered.at[my_summ],
                tok_send.at[at],
                tok_recv.at[my_summ],
                me,
                line(step) * CORES + core,
            )
        )
    sends.append(
        remote(tokens, gathered.at[my_summ], tok_send.at[3], tok_recv.at[my_summ], me, sibling)
    )
    for send in sends:
        send.start()

    def give(source, held, send_sem, recv_sem, space, summ):
        cols = pl.ds(pl.multiple_of(summ * LANES, LANES), LANES)
        remote(source.at[my_rows, cols], held.at[my_summ], send_sem, recv_sem, space, summ).start()

    def give_summary():
        for step in (1, -1):
            for to_core in range(CORES):
                give(sum_keys, keys, k_send, k_recv, *ring(step, to_core))
        for to_core in range(CORES):
            give(sum_keys, keys, k_send, k_recv, *ring(2, to_core))
        give(sum_keys, keys, k_send, k_recv, me, sibling)
        for step in (1, -1):
            for to_core in range(CORES):
                give(sum_values, values, v_send, v_recv, *ring(step, to_core))
        for to_core in range(CORES):
            give(sum_values, values, v_send, v_recv, *ring(-2, to_core))
        give(sum_values, values, v_send, v_recv, me, sibling)

    @pl.when(z_at < LATE_Z)
    def _():
        give_summary()

    lane = lax.broadcasted_iota(jnp.int32, inverse.shape, 1)

    def place(at, so_far):
        return so_far + jnp.where(lane == tile_map[at], at, 0)

    inverse[...] = lax.fori_loop(0, n_space, place, jnp.zeros(inverse.shape, jnp.int32))
    to_scalars = local(inverse, inverse_s, inverse_sem)
    to_scalars.start()

    loads[4].wait()

    def fill(at, carry):
        rows = pl.ds(pl.multiple_of(at * UNIT, UNIT), UNIT)
        code = codes[rows, :]
        first = jnp.full(code.shape, HIDDEN, jnp.float32)
        second = first
        for i in range(WIN):
            for j in range(WIN):
                here = code == i * WIN + j
                first = jnp.where(here, pos_bias[i, 0, j], first)
                second = jnp.where(here, pos_bias[i, 1, j], second)
        bias[0, rows, :] = first
        bias[1, rows, :] = second
        return carry

    lax.fori_loop(0, bias.shape[1] // UNIT, fill, 0)
    my_tile = tile_map[me]
    tile_row, tile_col = my_tile // TX, my_tile % TX
    edge = {
        (-1, 0): jnp.where(tile_row > 0, 0.0, HIDDEN),
        (1, 0): jnp.where(tile_row < ty - 1, 0.0, HIDDEN),
        (0, -1): jnp.where(tile_col > 0, 0.0, HIDDEN),
        (0, 1): jnp.where(tile_col < TX - 1, 0.0, HIDDEN),
    }
    for down in (-1, 1):
        for across in (-1, 1):
            edge[down, across] = jnp.minimum(edge[down, 0], edge[0, across])
    for step, hidden in edge.items():
        at = TOK + UNIT_STEP.index(step) * UNIT
        rows = slice(at, at + UNIT_STEP.count(step) * UNIT)
        for h in range(2):
            bias[h, rows, :] = bias[h, rows, :] + hidden

    forwards = []
    for at, step in enumerate((1, 3, 2)):
        slab = line(step) * CORES + core
        local(gathered.at[slab], gathered.at[slab], tok_recv.at[slab]).wait()
        forward = remote(
            gathered.at[slab],
            gathered.at[slab],
            tok_send.at[4 + at],
            tok_recv.at[slab],
            me,
            sibling,
        )
        forward.start()
        forwards.append(forward)
    own_tokens.wait()
    for step in range(YL):
        slab = line(step) * CORES + 1 - core
        local(gathered.at[slab], gathered.at[slab], tok_recv.at[slab]).wait()

    squares = jnp.zeros((TOK, LANES), jnp.float32)
    for slab in range(YL * CORES):
        floats = gathered[slab].astype(jnp.float32)
        squares = squares + floats * floats
    scale = lax.rsqrt(jnp.sum(squares, axis=-1, keepdims=True) * (1.0 / D) + EPSILON)
    for slab in range(YL * CORES):
        cols = slice(slab * LANES, (slab + 1) * LANES)
        floats = gathered[slab].astype(jnp.float32)
        normed[:, cols] = (floats * scale * gain[:, cols]).astype(jnp.bfloat16)
    for load in loads[:3]:
        load.wait()
    own_kv = jnp.dot(normed[...], weights[:, LANES:], preferred_element_type=jnp.float32)
    own_kv = own_kv.astype(jnp.bfloat16)
    own_k[...] = own_kv[:, :LANES]
    own_v = own_kv[:, LANES:]

    loads[5].wait()
    sides = jnp.dot(picks[...].astype(jnp.bfloat16), own_kv, preferred_element_type=jnp.float32)
    sides = sides.astype(jnp.bfloat16)
    for which in range(2):
        own = own_kv[:, which * LANES : (which + 1) * LANES]
        first = which * N_UNIT
        bands = BAND // UNIT
        pack[first : first + bands] = own[TOK - BAND :].reshape(bands, UNIT, LANES)
        pack[first + bands : first + 2 * bands] = own[:BAND].reshape(bands, UNIT, LANES)
        pack[first + 2 * bands : first + N_UNIT] = sides[
            :, which * LANES : (which + 1) * LANES
        ].reshape(N_UNIT - 2 * bands, UNIT, LANES)

    def send_rim(unit, carry):
        router = unit % n_space
        slot = unit // n_space

        @pl.when(router != me)
        def _():
            remote(
                pack.at[unit],
                routed.at[slot, me],
                rim_send,
                rim_recv.at[slot],
                router,
                my_summ,
            ).start()

        @pl.when(router == me)
        def _():
            local(pack.at[unit], routed.at[slot, me], rim_recv.at[slot]).start()

        return carry

    lax.fori_loop(0, 2 * N_UNIT, send_rim, 0)

    own_q = jnp.dot(normed[...], weights[:, :LANES], preferred_element_type=jnp.float32)
    scaled = own_q.astype(jnp.bfloat16).astype(jnp.float32) * HD ** (-0.5)
    queries[x_at] = scaled.T.astype(jnp.bfloat16)
    peers = [(x_at + step) % X for step in range(X)]
    for step in range(1, X):
        remote(
            queries.at[x_at],
            queries.at[x_at],
            q_send,
            q_recv.at[x_at],
            me - x_at + peers[step],
            my_summ,
        ).start()

    def one_head(both, h):
        blank = jnp.zeros((HD, TOK), jnp.bfloat16)
        own = both[h * HD : (h + 1) * HD]
        return jnp.concatenate([own, blank] if h == 0 else [blank, own], axis=0)

    def attend(scores, v_rows):
        top = jnp.max(scores, axis=0, keepdims=True)
        weight = jnp.exp(scores - top)
        total = jnp.sum(weight, axis=0, keepdims=True)
        summed = jnp.dot(v_rows, weight.astype(jnp.bfloat16), preferred_element_type=jnp.float32)
        return top, total, summed

    my_queries = queries[x_at]
    own_vt = own_v.astype(jnp.float32).T.astype(jnp.bfloat16)
    parts = [[], []]
    for h in range(2):
        scores = jnp.dot(own_k[...], one_head(my_queries, h), preferred_element_type=jnp.float32)
        parts[h].append(attend(scores + bias[h, :TOK], own_vt[h * HD : (h + 1) * HD]))

    @pl.when(z_at >= LATE_Z)
    def _():
        give_summary()

    local(values, values, v_recv).wait()
    for slab in range(YL * CORES):
        values_t[:, slab * share : (slab + 1) * share] = (
            values[slab].astype(jnp.float32).T.astype(jnp.bfloat16)
        )
    local(keys, keys, k_recv).wait()

    def summary(step, carry):
        peer = (x_at + step) % X

        @pl.when(step > 0)
        def _():
            local(queries.at[peer], queries.at[peer], q_recv.at[peer]).wait()

        theirs = queries[peer]
        key_rows = keys[...].reshape(YL * CORES * share, LANES)
        tops, totals, sums = [], [], []
        for h in range(2):
            scores = jnp.dot(key_rows, one_head(theirs, h), preferred_element_type=jnp.float32)
            top, total, summed = attend(scores, values_t[h * HD : (h + 1) * HD, :])
            tops.append(top)
            totals.append(total)
            sums.append(summed)
        part_out[peer] = jnp.concatenate(sums, axis=0).astype(jnp.bfloat16)
        stat_out[peer] = jnp.concatenate(tops + totals + [jnp.zeros((4, TOK), jnp.float32)], axis=0)

        @pl.when(step > 0)
        def _():
            to = me - x_at + peer
            remote(
                part_out.at[peer], part_in.at[x_at], part_send, part_recv.at[x_at], to, my_summ
            ).start()
            remote(
                stat_out.at[peer], stat_in.at[x_at], stat_send, stat_recv.at[x_at], to, my_summ
            ).start()

        return carry

    lax.fori_loop(0, X, summary, 0)

    to_scalars.wait()
    for slot in range(slots):
        unit = me + slot * n_space

        @pl.when(unit < 2 * N_UNIT)
        def _():
            local(routed.at[slot], routed.at[slot], rim_recv.at[slot]).wait()
            kind = unit % N_UNIT
            down = jnp.where(
                kind < 6, -1, jnp.where(kind < 12, 1, jnp.where(kind < 16, 0, jnp.where(kind < 18, -1, 1)))
            )
            across = jnp.where(
                kind < 12,
                0,
                jnp.where(kind < 14, -1, jnp.where(kind < 16, 1, jnp.where(kind % 2 == 0, -1, 1))),
            )

            def pass_on(to, carry):
                tile = tile_map[to]
                row = jnp.clip(tile // TX + down, 0, ty - 1)
                col = jnp.clip(tile % TX + across, 0, TX - 1)
                holder = jnp.clip(inverse_s[0, row * TX + col], 0, n_space - 1)
                staged[slot, to] = routed[slot, holder]

                @pl.when(to != me)
                def _():
                    remote(
                        staged.at[slot, to], halo.at[unit], halo_send, halo_recv, to, my_summ
                    ).start()

                @pl.when(to == me)
                def _():
                    local(staged.at[slot, to], halo.at[unit], halo_recv).start()

                return carry

            lax.fori_loop(0, n_space, pass_on, 0)

    local(halo, halo, halo_recv).wait()
    halo_k = halo[:N_UNIT].reshape(HALO_KEYS, LANES)
    halo_vt = halo[N_UNIT:].reshape(HALO_KEYS, LANES).astype(jnp.float32).T.astype(jnp.bfloat16)
    for h in range(2):
        scores = jnp.dot(halo_k, one_head(my_queries, h), preferred_element_type=jnp.float32)
        parts[h].append(attend(scores + bias[h, TOK:], halo_vt[h * HD : (h + 1) * HD]))

    for step in range(X):
        peer = peers[step]
        if step > 0:
            local(part_in.at[peer], part_in.at[peer], part_recv.at[peer]).wait()
            local(stat_in.at[peer], stat_in.at[peer], stat_recv.at[peer]).wait()
            rows, stats = part_in[peer], stat_in[peer]
        else:
            rows, stats = part_out[peer], stat_out[peer]
        for h in range(2):
            parts[h].append(
                (
                    stats[h : h + 1],
                    stats[2 + h : 3 + h],
                    rows[h * HD : (h + 1) * HD].astype(jnp.float32),
                )
            )
    heads = []
    for h in range(2):
        joint = parts[h][0][0]
        for top, _, _ in parts[h][1:]:
            joint = jnp.maximum(joint, top)
        total = jnp.zeros((1, TOK), jnp.float32)
        summed = jnp.zeros((HD, TOK), jnp.float32)
        for top, part_total, part_sum in parts[h]:
            factor = jnp.exp(top - joint)
            total = total + part_total * factor
            summed = summed + part_sum * factor
        heads.append(summed / total)
    attended = jnp.concatenate(heads, axis=0).T.astype(jnp.bfloat16)

    loads[3].wait()
    mixed = jnp.dot(attended, out_w[...], preferred_element_type=jnp.float32).astype(jnp.bfloat16)
    for at in range(YL):
        for side in range(CORES):
            slab = at * CORES + side
            terms[side, at] = mixed[:, slab * LANES : (slab + 1) * LANES]
    order = [line(step) for step in (2, 1, 3, 0)]
    pair = []
    for at in order:
        pair.append(
            remote(
                terms.at[1 - core, at], pair_in.at[at], pair_send.at[at], pair_recv.at[at], me, sibling
            )
        )
        pair[-1].start()
    along = []
    for at in order[:3]:
        local(pair_in.at[at], pair_in.at[at], pair_recv.at[at]).wait()
        both = terms[core, at].astype(jnp.float32) + pair_in[at].astype(jnp.float32)
        pair_sum[at] = both.astype(jnp.bfloat16)
        along.append(
            remote(
                pair_sum.at[at],
                line_in.at[y_lo],
                line_send.at[at],
                line_recv.at[y_lo],
                me,
                at * CORES + core,
            )
        )
        along[-1].start()
    local(pair_in.at[y_lo], pair_in.at[y_lo], pair_recv.at[y_lo]).wait()
    result = terms[core, y_lo].astype(jnp.float32) + pair_in[y_lo].astype(jnp.float32)
    for step in (1, 3, 2):
        at = line(step)
        local(line_in.at[at], line_in.at[at], line_recv.at[at]).wait()
        result = result + line_in[at].astype(jnp.float32)
    out[...] = result.astype(jnp.bfloat16)

    for send in sends + forwards + pair + along:
        send.wait_send()
    for sem, held in ((k_send, keys), (v_send, values)):
        sent = held.at[: YL * CORES - 1]
        local(sent, sent, sem).wait()
    for sem, held in ((q_send, queries), (part_send, part_out), (stat_send, stat_out)):
        sent = held.at[: X - 1]
        local(sent, sent, sem).wait()
    routers = [unit % n_space for unit in range(2 * N_UNIT)]
    own_units = jnp.where(me < (2 * N_UNIT) % n_space, 1, 0) + 2 * N_UNIT // n_space
    for count in sorted({routers.count(at) for at in range(n_space)}):

        @pl.when(own_units == count)
        def _():
            sent = pack.at[: 2 * N_UNIT - count]
            local(sent, sent, rim_send).wait()

    for slot in range(slots):

        @pl.when(me + slot * n_space < 2 * N_UNIT)
        def _():
            sent = staged.at[slot, : n_space - 1]
            local(sent, sent, halo_send).wait()


def shards(
    n_space,
    tokens,
    tile_map,
    norm_gain,
    q_weight,
    k_weight,
    v_weight,
    out_weight,
    pos_bias,
    sum_keys,
    sum_values,
):
    share = sum_keys.shape[0] // X
    slots = -(-2 * N_UNIT // n_space)
    bf16 = jnp.bfloat16
    f32 = jnp.float32
    dma = pltpu.SemaphoreType.DMA
    anywhere = pl.BlockSpec(memory_space=pl.ANY)
    scalars = pl.BlockSpec(memory_space=pltpu.SMEM)
    vector = pl.BlockSpec(memory_space=pltpu.VMEM)
    slab = (TOK, LANES)
    turned = (LANES, TOK)
    scratch = [
        pltpu.VMEM((YL * CORES,) + slab, bf16),
        pltpu.VMEM((TOK, D), bf16),
        pltpu.VMEM((D, 3 * LANES), bf16),
        pltpu.VMEM((LANES, D), bf16),
        pltpu.VMEM((TOK + HALO_KEYS, TOK), jnp.int32),
        pltpu.VMEM((SIDE_ROWS, TOK), f32),
        pltpu.VMEM((2, TOK + HALO_KEYS, TOK), f32),
        pltpu.VMEM(slab, bf16),
        pltpu.VMEM((YL * CORES, share, LANES), bf16),
        pltpu.VMEM((YL * CORES, share, LANES), bf16),
        pltpu.VMEM((LANES, YL * CORES * share), bf16),
        pltpu.VMEM((X,) + turned, bf16),
        pltpu.VMEM((X,) + turned, bf16),
        pltpu.VMEM((X,) + turned, bf16),
        pltpu.VMEM((X, 8, TOK), f32),
        pltpu.VMEM((X, 8, TOK), f32),
        pltpu.VMEM((8, LANES), jnp.int32),
        pltpu.SMEM((8, LANES), jnp.int32),
        pltpu.VMEM((2 * N_UNIT, UNIT, LANES), bf16),
        pltpu.VMEM((slots, n_space, UNIT, LANES), bf16),
        pltpu.VMEM((slots, n_space, UNIT, LANES), bf16),
        pltpu.VMEM((2 * N_UNIT, UNIT, LANES), bf16),
        pltpu.VMEM((CORES, YL) + slab, bf16),
        pltpu.VMEM((YL,) + slab, bf16),
        pltpu.VMEM((YL,) + slab, bf16),
        pltpu.VMEM((YL,) + slab, bf16),
        dma((6,)),
        dma,
        dma((7,)),
        dma((YL * CORES,)),
        dma,
        dma,
        dma,
        dma,
        dma,
        dma((X,)),
        dma,
        dma((X,)),
        dma,
        dma((X,)),
        dma,
        dma((slots,)),
        dma,
        dma,
        dma((YL,)),
        dma((YL,)),
        dma((YL,)),
        dma((YL,)),
    ]
    mixed = pl.pallas_call(
        partial(kernel, n_space),
        out_shape=jax.ShapeDtypeStruct(slab, bf16),
        in_specs=[scalars, scalars, anywhere, vector] + [anywhere] * 8,
        out_specs=vector,
        scratch_shapes=scratch,
        compiler_params=pltpu.CompilerParams(
            collective_id=0, has_side_effects=True, vmem_limit_bytes=63 * 1024 * 1024
        ),
        name="tile_attention",
    )(
        tile_map,
        pos_bias.transpose(1, 0, 2),
        tokens.reshape(slab),
        norm_gain.reshape(1, D),
        q_weight,
        k_weight,
        v_weight,
        out_weight,
        sum_keys,
        sum_values,
        jnp.asarray(offset_codes()),
        jnp.asarray(side_picks()),
    )
    return mixed.reshape(1, BH, BW, LANES)


def solution(mesh):
    return jax.shard_map(
        partial(shards, mesh.shape["space"]),
        mesh=mesh,
        in_specs=(
            P("space", None, None, "summ"),
            P(),
            P(),
            P(None, "summ"),
            P(None, "summ"),
            P(None, "summ"),
            P("summ", None),
            P("summ", None, None),
            P("summ", None),
            P("summ", None),
        ),
        out_specs=P("space", None, None, "summ"),
        check_vma=False,
    )
```

```python
from functools import partial

import numpy as np
import jax
import jax.numpy as jnp
from jax import lax
from jax.experimental import pallas as pl
from jax.experimental.pallas import tpu as pltpu
from jax.sharding import PartitionSpec as P

D = 1024
HD = 64
HALO = 3
TX = 8
BW = 32
BH = 8
EPSILON = 1e-05
WIN = 2 * HALO + 1
TOK = BH * BW
LANES = 128
X = 4
YH = 2
YL = 4
CORES = 2
HIDDEN = -1e30
UNIT = 16
UNIT_STEP = (
    [(-1, 0)] * 6
    + [(1, 0)] * 6
    + [(0, -1)] * 2
    + [(0, 1)] * 2
    + [(-1, -1), (-1, 1), (1, -1), (1, 1)]
)
N_UNIT = len(UNIT_STEP)
HALO_KEYS = N_UNIT * UNIT
BAND = HALO * BW
SIDE_ROWS = HALO_KEYS - 2 * BAND
LATE_Z = 4
MESH = pl.DeviceIdType.MESH


def halo_positions():
    places = [(-HALO + j // BW, j % BW, (BH - HALO) * BW + j) for j in range(BAND)]
    places += [(BH + j // BW, j % BW, j) for j in range(BAND)]

    def side(count, rows, padded, row_at, col_at, from_row, from_col):
        out = []
        for i in range(padded):
            r, c = i // HALO, i % HALO
            out.append((row_at + r, col_at + c, (from_row + r) * BW + from_col + c) if i < count else None)
        return out

    places += side(BH * HALO, BH, 2 * UNIT, 0, -HALO, 0, BW - HALO)
    places += side(BH * HALO, BH, 2 * UNIT, 0, BW, 0, 0)
    places += side(HALO * HALO, HALO, UNIT, -HALO, -HALO, BH - HALO, BW - HALO)
    places += side(HALO * HALO, HALO, UNIT, -HALO, BW, BH - HALO, 0)
    places += side(HALO * HALO, HALO, UNIT, BH, -HALO, 0, BW - HALO)
    places += side(HALO * HALO, HALO, UNIT, BH, BW, 0, 0)
    return places


def offset_codes():
    keys = [(k // BW, k % BW) for k in range(TOK)]
    keys += [(None if place is None else place[:2]) for place in halo_positions()]
    codes = np.full((len(keys), TOK), -1, np.int32)
    rows, cols = np.arange(TOK) // BW, np.arange(TOK) % BW
    for at, key in enumerate(keys):
        if key is None:
            continue
        i, j = key[0] - rows + HALO, key[1] - cols + HALO
        near = (i >= 0) & (i < WIN) & (j >= 0) & (j < WIN)
        codes[at] = np.where(near, i * WIN + j, -1)
    return codes


def side_picks():
    picks = np.zeros((SIDE_ROWS, TOK), np.float32)
    for at, place in enumerate(halo_positions()[2 * BAND :]):
        if place is not None:
            picks[at, place[2]] = 1.0
    return picks


def kernel(
    n_space,
    tile_map,
    pos_bias,
    tokens,
    gain,
    q_weight,
    k_weight,
    v_weight,
    out_weight,
    sum_keys,
    sum_values,
    codes_in,
    picks_in,
    out,
    gathered,
    normed,
    weights,
    out_w,
    codes,
    picks,
    bias,
    own_k,
    keys,
    values,
    values_t,
    queries,
    part_out,
    part_in,
    stat_out,
    stat_in,
    inverse,
    inverse_s,
    pack,
    routed,
    staged,
    halo,
    terms,
    pair_in,
    pair_sum,
    line_in,
    load_sem,
    inverse_sem,
    entered,
    tok_send,
    tok_recv,
    k_send,
    k_recv,
    v_send,
    v_recv,
    q_send,
    q_recv,
    part_send,
    part_recv,
    stat_send,
    stat_recv,
    rim_send,
    rim_recv,
    halo_send,
    halo_recv,
    pair_send,
    pair_recv,
    line_send,
    line_recv,
):
    slots = routed.shape[0]
    hub = n_space - 1
    share = keys.shape[1]
    ty = n_space // TX
    me = lax.axis_index("space")
    my_summ = lax.axis_index("summ")
    y_lo, core = my_summ // CORES, my_summ % CORES
    x_at = me % X
    y_hi = (me // X) % YH
    z_at = me // (X * YH)
    y_at = y_hi * YL + y_lo
    sibling = y_lo * CORES + 1 - core

    def local(src, dst, sem):
        return pltpu.make_async_copy(src, dst, sem)

    def remote(src, dst, send, recv, space, summ):
        return pltpu.make_async_remote_copy(
            src_ref=src,
            dst_ref=dst,
            send_sem=send,
            recv_sem=recv,
            device_id=(space, summ),
            device_id_type=MESH,
        )

    def ring(step, to_core):
        y = (y_at + step + YH * YL) % (YH * YL)
        return (z_at * YH + y // YL) * X + x_at, (y % YL) * CORES + to_core

    def line(step):
        return (y_lo + step) % YL

    barrier = pltpu.get_barrier_semaphore()

    def greet(space, summ):
        pl.semaphore_signal(barrier, inc=1, device_id=(space, summ), device_id_type=MESH)

    greet(me, sibling)
    for step in range(1, YL):
        greet(me, line(step) * CORES + core)
    for step in (1, -1, 2, -2):
        for to_core in range(CORES):
            greet(*ring(step, to_core))

    for step in range(1, X):
        greet(me - x_at + (x_at + step) % X, my_summ)

    @pl.when(me != hub)
    def _():
        greet(hub, my_summ)

    loads = [
        local(codes_in, codes, load_sem.at[0]),
        local(k_weight, weights.at[:, LANES : 2 * LANES], load_sem.at[1]),
        local(v_weight, weights.at[:, 2 * LANES : 3 * LANES], load_sem.at[2]),
        local(q_weight, weights.at[:, 0:LANES], load_sem.at[3]),
        local(picks_in, picks, load_sem.at[4]),
        local(out_weight, out_w, load_sem.at[5]),
    ]
    own_tokens = local(tokens, gathered.at[my_summ], tok_recv.at[my_summ])
    own_tokens.start()
    for load in loads:
        load.start()
    my_rows = pl.ds(pl.multiple_of(x_at * share, share), share)
    my_cols = pl.ds(pl.multiple_of(my_summ * LANES, LANES), LANES)
    local(sum_keys.at[my_rows, my_cols], keys.at[my_summ], k_recv).start()
    local(sum_values.at[my_rows, my_cols], values.at[my_summ], v_recv).start()

    to_scalars = local(inverse, inverse_s, inverse_sem)

    def prepare():
        lane = lax.broadcasted_iota(jnp.int32, inverse.shape, 1)

        def place(at, so_far):
            return so_far + jnp.where(lane == tile_map[at], at, 0)

        inverse[...] = lax.fori_loop(0, n_space, place, jnp.zeros(inverse.shape, jnp.int32))
        to_scalars.start()

        loads[0].wait()

        def fill(at, carry):
            rows = pl.ds(pl.multiple_of(at * UNIT, UNIT), UNIT)
            code = codes[rows, :]
            first = jnp.full(code.shape, HIDDEN, jnp.float32)
            second = first
            for i in range(WIN):
                for j in range(WIN):
                    here = code == i * WIN + j
                    first = jnp.where(here, pos_bias[i, 0, j], first)
                    second = jnp.where(here, pos_bias[i, 1, j], second)
            bias[0, rows, :] = first
            bias[1, rows, :] = second
            return carry

        lax.fori_loop(0, bias.shape[1] // UNIT, fill, 0)
        my_tile = tile_map[me]
        tile_row, tile_col = my_tile // TX, my_tile % TX
        edge = {
            (-1, 0): jnp.where(tile_row > 0, 0.0, HIDDEN),
            (1, 0): jnp.where(tile_row < ty - 1, 0.0, HIDDEN),
            (0, -1): jnp.where(tile_col > 0, 0.0, HIDDEN),
            (0, 1): jnp.where(tile_col < TX - 1, 0.0, HIDDEN),
        }
        for down in (-1, 1):
            for across in (-1, 1):
                edge[down, across] = jnp.minimum(edge[down, 0], edge[0, across])
        for step, hidden in edge.items():
            at = TOK + UNIT_STEP.index(step) * UNIT
            rows = slice(at, at + UNIT_STEP.count(step) * UNIT)
            for h in range(2):
                bias[h, rows, :] = bias[h, rows, :] + hidden

    @pl.when(z_at < LATE_Z)
    def _():
        prepare()

    near = 1 + (YL - 1) + 4 * CORES + (X - 1)
    pl.semaphore_wait(barrier, near + jnp.where(me == hub, n_space - 1, 0))

    @pl.when(me == hub)
    def _():
        def tell(step, carry):
            pl.semaphore_signal(
                entered,
                inc=1,
                device_id=((me + step) % n_space, my_summ),
                device_id_type=MESH,
            )
            return carry

        lax.fori_loop(1, n_space, tell, 0)

    sends = []
    for at, step in enumerate((2, 1, 3)):
        sends.append(
            remote(
                tokens,
                gathered.at[my_summ],
                tok_send.at[at],
                tok_recv.at[my_summ],
                me,
                line(step) * CORES + core,
            )
        )
    sends.append(
        remote(tokens, gathered.at[my_summ], tok_send.at[3], tok_recv.at[my_summ], me, sibling)
    )
    for send in sends:
        send.start()

    def give(source, held, send_sem, recv_sem, space, summ):
        cols = pl.ds(pl.multiple_of(summ * LANES, LANES), LANES)
        remote(source.at[my_rows, cols], held.at[my_summ], send_sem, recv_sem, space, summ).start()

    def give_summary():
        for step in (1, -1):
            for to_core in range(CORES):
                give(sum_keys, keys, k_send, k_recv, *ring(step, to_core))
        for to_core in range(CORES):
            give(sum_keys, keys, k_send, k_recv, *ring(2, to_core))
        give(sum_keys, keys, k_send, k_recv, me, sibling)
        for step in (1, -1):
            for to_core in range(CORES):
                give(sum_values, values, v_send, v_recv, *ring(step, to_core))
        for to_core in range(CORES):
            give(sum_values, values, v_send, v_recv, *ring(-2, to_core))
        give(sum_values, values, v_send, v_recv, me, sibling)

    @pl.when(z_at < LATE_Z)
    def _():
        give_summary()

    forwards = []
    for at, step in enumerate((1, 3, 2)):
        slab = line(step) * CORES + core
        local(gathered.at[slab], gathered.at[slab], tok_recv.at[slab]).wait()
        forward = remote(
            gathered.at[slab],
            gathered.at[slab],
            tok_send.at[4 + at],
            tok_recv.at[slab],
            me,
            sibling,
        )
        forward.start()
        forwards.append(forward)
    own_tokens.wait()
    for step in range(YL):
        slab = line(step) * CORES + 1 - core
        local(gathered.at[slab], gathered.at[slab], tok_recv.at[slab]).wait()

    squares = jnp.zeros((TOK, LANES), jnp.float32)
    for slab in range(YL * CORES):
        floats = gathered[slab].astype(jnp.float32)
        squares = squares + floats * floats
    scale = lax.rsqrt(jnp.sum(squares, axis=-1, keepdims=True) * (1.0 / D) + EPSILON)
    for slab in range(YL * CORES):
        cols = slice(slab * LANES, (slab + 1) * LANES)
        floats = gathered[slab].astype(jnp.float32)
        normed[:, cols] = (floats * scale * gain[:, cols]).astype(jnp.bfloat16)
    for load in loads[1:3]:
        load.wait()
    own_kv = jnp.dot(normed[...], weights[:, LANES:], preferred_element_type=jnp.float32)
    own_kv = own_kv.astype(jnp.bfloat16)
    own_k[...] = own_kv[:, :LANES]
    own_v = own_kv[:, LANES:]

    loads[4].wait()
    sides = jnp.dot(picks[...].astype(jnp.bfloat16), own_kv, preferred_element_type=jnp.float32)
    sides = sides.astype(jnp.bfloat16)
    for which in range(2):
        own = own_kv[:, which * LANES : (which + 1) * LANES]
        first = which * N_UNIT
        bands = BAND // UNIT
        pack[first : first + bands] = own[TOK - BAND :].reshape(bands, UNIT, LANES)
        pack[first + bands : first + 2 * bands] = own[:BAND].reshape(bands, UNIT, LANES)
        pack[first + 2 * bands : first + N_UNIT] = sides[
            :, which * LANES : (which + 1) * LANES
        ].reshape(N_UNIT - 2 * bands, UNIT, LANES)

    def send_rim(unit, carry):
        router = unit % n_space
        slot = unit // n_space

        @pl.when(router != me)
        def _():
            remote(
                pack.at[unit],
                routed.at[slot, me],
                rim_send,
                rim_recv.at[slot],
                router,
                my_summ,
            ).start()

        @pl.when(router == me)
        def _():
            local(pack.at[unit], routed.at[slot, me], rim_recv.at[slot]).start()

        return carry

    @pl.when(me != hub)
    def _():
        pl.semaphore_wait(entered, 1)

    lax.fori_loop(0, 2 * N_UNIT, send_rim, 0)

    loads[3].wait()
    own_q = jnp.dot(normed[...], weights[:, :LANES], preferred_element_type=jnp.float32)
    scaled = own_q.astype(jnp.bfloat16).astype(jnp.float32) * HD ** (-0.5)
    queries[x_at] = scaled.T.astype(jnp.bfloat16)
    peers = [(x_at + step) % X for step in range(X)]
    for step in range(1, X):
        remote(
            queries.at[x_at],
            queries.at[x_at],
            q_send,
            q_recv.at[x_at],
            me - x_at + peers[step],
            my_summ,
        ).start()

    def one_head(both, h):
        blank = jnp.zeros((HD, TOK), jnp.bfloat16)
        own = both[h * HD : (h + 1) * HD]
        return jnp.concatenate([own, blank] if h == 0 else [blank, own], axis=0)

    def attend(scores, v_rows):
        top = jnp.max(scores, axis=0, keepdims=True)
        weight = jnp.exp(scores - top)
        total = jnp.sum(weight, axis=0, keepdims=True)
        summed = jnp.dot(v_rows, weight.astype(jnp.bfloat16), preferred_element_type=jnp.float32)
        return top, total, summed

    @pl.when(z_at >= LATE_Z)
    def _():
        prepare()

    my_queries = queries[x_at]
    own_vt = own_v.astype(jnp.float32).T.astype(jnp.bfloat16)
    parts = [[], []]
    for h in range(2):
        scores = jnp.dot(own_k[...], one_head(my_queries, h), preferred_element_type=jnp.float32)
        parts[h].append(attend(scores + bias[h, :TOK], own_vt[h * HD : (h + 1) * HD]))

    to_scalars.wait()

    def route():
        for slot in range(slots):
            unit = me + slot * n_space

            @pl.when(unit < 2 * N_UNIT)
            def _():
                local(routed.at[slot], routed.at[slot], rim_recv.at[slot]).wait()
                kind = unit % N_UNIT
                down = jnp.where(
                    kind < 6, -1, jnp.where(kind < 12, 1, jnp.where(kind < 16, 0, jnp.where(kind < 18, -1, 1)))
                )
                across = jnp.where(
                    kind < 12,
                    0,
                    jnp.where(kind < 14, -1, jnp.where(kind < 16, 1, jnp.where(kind % 2 == 0, -1, 1))),
                )

                def pass_on(to, carry):
                    tile = tile_map[to]
                    row = jnp.clip(tile // TX + down, 0, ty - 1)
                    col = jnp.clip(tile % TX + across, 0, TX - 1)
                    holder = jnp.clip(inverse_s[0, row * TX + col], 0, n_space - 1)
                    staged[slot, to] = routed[slot, holder]

                    @pl.when(to != me)
                    def _():
                        remote(
                            staged.at[slot, to], halo.at[unit], halo_send, halo_recv, to, my_summ
                        ).start()

                    @pl.when(to == me)
                    def _():
                        local(staged.at[slot, to], halo.at[unit], halo_recv).start()

                    return carry

                lax.fori_loop(0, n_space, pass_on, 0)

    @pl.when(z_at >= LATE_Z)
    def _():
        route()

    @pl.when(z_at >= LATE_Z)
    def _():
        give_summary()

    local(values, values, v_recv).wait()
    for slab in range(YL * CORES):
        values_t[:, slab * share : (slab + 1) * share] = (
            values[slab].astype(jnp.float32).T.astype(jnp.bfloat16)
        )
    local(keys, keys, k_recv).wait()

    def summary(step, carry):
        peer = (x_at + step) % X

        @pl.when(step > 0)
        def _():
            local(queries.at[peer], queries.at[peer], q_recv.at[peer]).wait()

        theirs = queries[peer]
        key_rows = keys[...].reshape(YL * CORES * share, LANES)
        tops, totals, sums = [], [], []
        for h in range(2):
            scores = jnp.dot(key_rows, one_head(theirs, h), preferred_element_type=jnp.float32)
            top, total, summed = attend(scores, values_t[h * HD : (h + 1) * HD, :])
            tops.append(top)
            totals.append(total)
            sums.append(summed)
        part_out[peer] = jnp.concatenate(sums, axis=0).astype(jnp.bfloat16)
        stat_out[peer] = jnp.concatenate(tops + totals + [jnp.zeros((4, TOK), jnp.float32)], axis=0)

        @pl.when(step > 0)
        def _():
            to = me - x_at + peer
            remote(
                part_out.at[peer], part_in.at[x_at], part_send, part_recv.at[x_at], to, my_summ
            ).start()
            remote(
                stat_out.at[peer], stat_in.at[x_at], stat_send, stat_recv.at[x_at], to, my_summ
            ).start()

        return carry

    lax.fori_loop(0, X, summary, 0)

    @pl.when(z_at < LATE_Z)
    def _():
        route()

    local(halo, halo, halo_recv).wait()
    halo_k = halo[:N_UNIT].reshape(HALO_KEYS, LANES)
    halo_vt = halo[N_UNIT:].reshape(HALO_KEYS, LANES).astype(jnp.float32).T.astype(jnp.bfloat16)
    for h in range(2):
        scores = jnp.dot(halo_k, one_head(my_queries, h), preferred_element_type=jnp.float32)
        parts[h].append(attend(scores + bias[h, TOK:], halo_vt[h * HD : (h + 1) * HD]))

    for step in range(X):
        peer = peers[step]
        if step > 0:
            local(part_in.at[peer], part_in.at[peer], part_recv.at[peer]).wait()
            local(stat_in.at[peer], stat_in.at[peer], stat_recv.at[peer]).wait()
            rows, stats = part_in[peer], stat_in[peer]
        else:
            rows, stats = part_out[peer], stat_out[peer]
        for h in range(2):
            parts[h].append(
                (
                    stats[h : h + 1],
                    stats[2 + h : 3 + h],
                    rows[h * HD : (h + 1) * HD].astype(jnp.float32),
                )
            )
    heads = []
    for h in range(2):
        joint = parts[h][0][0]
        for top, _, _ in parts[h][1:]:
            joint = jnp.maximum(joint, top)
        total = jnp.zeros((1, TOK), jnp.float32)
        summed = jnp.zeros((HD, TOK), jnp.float32)
        for top, part_total, part_sum in parts[h]:
            factor = jnp.exp(top - joint)
            total = total + part_total * factor
            summed = summed + part_sum * factor
        heads.append(summed / total)
    attended = jnp.concatenate(heads, axis=0).T.astype(jnp.bfloat16)

    loads[5].wait()
    mixed = jnp.dot(attended, out_w[...], preferred_element_type=jnp.float32).astype(jnp.bfloat16)
    for at in range(YL):
        for side in range(CORES):
            slab = at * CORES + side
            terms[side, at] = mixed[:, slab * LANES : (slab + 1) * LANES]
    order = [line(step) for step in (2, 1, 3, 0)]
    pair = []
    for at in order:
        pair.append(
            remote(
                terms.at[1 - core, at], pair_in.at[at], pair_send.at[at], pair_recv.at[at], me, sibling
            )
        )
        pair[-1].start()
    along = []
    for at in order[:3]:
        local(pair_in.at[at], pair_in.at[at], pair_recv.at[at]).wait()
        both = terms[core, at].astype(jnp.float32) + pair_in[at].astype(jnp.float32)
        pair_sum[at] = both.astype(jnp.bfloat16)
        along.append(
            remote(
                pair_sum.at[at],
                line_in.at[y_lo],
                line_send.at[at],
                line_recv.at[y_lo],
                me,
                at * CORES + core,
            )
        )
        along[-1].start()
    local(pair_in.at[y_lo], pair_in.at[y_lo], pair_recv.at[y_lo]).wait()
    result = terms[core, y_lo].astype(jnp.float32) + pair_in[y_lo].astype(jnp.float32)
    for step in (1, 3, 2):
        at = line(step)
        local(line_in.at[at], line_in.at[at], line_recv.at[at]).wait()
        result = result + line_in[at].astype(jnp.float32)
    out[...] = result.astype(jnp.bfloat16)

    for send in sends + forwards + pair + along:
        send.wait_send()
    for sem, held in ((k_send, keys), (v_send, values)):
        sent = held.at[: YL * CORES - 1]
        local(sent, sent, sem).wait()
    for sem, held in ((q_send, queries), (part_send, part_out), (stat_send, stat_out)):
        sent = held.at[: X - 1]
        local(sent, sent, sem).wait()
    routers = [unit % n_space for unit in range(2 * N_UNIT)]
    own_units = jnp.where(me < (2 * N_UNIT) % n_space, 1, 0) + 2 * N_UNIT // n_space
    for count in sorted({routers.count(at) for at in range(n_space)}):

        @pl.when(own_units == count)
        def _():
            sent = pack.at[: 2 * N_UNIT - count]
            local(sent, sent, rim_send).wait()

    for slot in range(slots):

        @pl.when(me + slot * n_space < 2 * N_UNIT)
        def _():
            sent = staged.at[slot, : n_space - 1]
            local(sent, sent, halo_send).wait()


def shards(
    n_space,
    tokens,
    tile_map,
    norm_gain,
    q_weight,
    k_weight,
    v_weight,
    out_weight,
    pos_bias,
    sum_keys,
    sum_values,
):
    share = sum_keys.shape[0] // X
    slots = -(-2 * N_UNIT // n_space)
    bf16 = jnp.bfloat16
    f32 = jnp.float32
    dma = pltpu.SemaphoreType.DMA
    anywhere = pl.BlockSpec(memory_space=pl.ANY)
    scalars = pl.BlockSpec(memory_space=pltpu.SMEM)
    vector = pl.BlockSpec(memory_space=pltpu.VMEM)
    slab = (TOK, LANES)
    turned = (LANES, TOK)
    scratch = [
        pltpu.VMEM((YL * CORES,) + slab, bf16),
        pltpu.VMEM((TOK, D), bf16),
        pltpu.VMEM((D, 3 * LANES), bf16),
        pltpu.VMEM((LANES, D), bf16),
        pltpu.VMEM((TOK + HALO_KEYS, TOK), jnp.int32),
        pltpu.VMEM((SIDE_ROWS, TOK), f32),
        pltpu.VMEM((2, TOK + HALO_KEYS, TOK), f32),
        pltpu.VMEM(slab, bf16),
        pltpu.VMEM((YL * CORES, share, LANES), bf16),
        pltpu.VMEM((YL * CORES, share, LANES), bf16),
        pltpu.VMEM((LANES, YL * CORES * share), bf16),
        pltpu.VMEM((X,) + turned, bf16),
        pltpu.VMEM((X,) + turned, bf16),
        pltpu.VMEM((X,) + turned, bf16),
        pltpu.VMEM((X, 8, TOK), f32),
        pltpu.VMEM((X, 8, TOK), f32),
        pltpu.VMEM((8, LANES), jnp.int32),
        pltpu.SMEM((8, LANES), jnp.int32),
        pltpu.VMEM((2 * N_UNIT, UNIT, LANES), bf16),
        pltpu.VMEM((slots, n_space, UNIT, LANES), bf16),
        pltpu.VMEM((slots, n_space, UNIT, LANES), bf16),
        pltpu.VMEM((2 * N_UNIT, UNIT, LANES), bf16),
        pltpu.VMEM((CORES, YL) + slab, bf16),
        pltpu.VMEM((YL,) + slab, bf16),
        pltpu.VMEM((YL,) + slab, bf16),
        pltpu.VMEM((YL,) + slab, bf16),
        dma((6,)),
        dma,
        pltpu.SemaphoreType.REGULAR,
        dma((7,)),
        dma((YL * CORES,)),
        dma,
        dma,
        dma,
        dma,
        dma,
        dma((X,)),
        dma,
        dma((X,)),
        dma,
        dma((X,)),
        dma,
        dma((slots,)),
        dma,
        dma,
        dma((YL,)),
        dma((YL,)),
        dma((YL,)),
        dma((YL,)),
    ]
    mixed = pl.pallas_call(
        partial(kernel, n_space),
        out_shape=jax.ShapeDtypeStruct(slab, bf16),
        in_specs=[scalars, scalars, anywhere, vector] + [anywhere] * 8,
        out_specs=vector,
        scratch_shapes=scratch,
        compiler_params=pltpu.CompilerParams(
            collective_id=0, has_side_effects=True, vmem_limit_bytes=63 * 1024 * 1024
        ),
        name="tile_attention",
    )(
        tile_map,
        pos_bias.transpose(1, 0, 2),
        tokens.reshape(slab),
        norm_gain.reshape(1, D),
        q_weight,
        k_weight,
        v_weight,
        out_weight,
        sum_keys,
        sum_values,
        jnp.asarray(offset_codes()),
        jnp.asarray(side_picks()),
    )
    return mixed.reshape(1, BH, BW, LANES)


def solution(mesh):
    return jax.shard_map(
        partial(shards, mesh.shape["space"]),
        mesh=mesh,
        in_specs=(
            P("space", None, None, "summ"),
            P(),
            P(),
            P(None, "summ"),
            P(None, "summ"),
            P(None, "summ"),
            P("summ", None),
            P("summ", None, None),
            P("summ", None),
            P("summ", None),
        ),
        out_specs=P("space", None, None, "summ"),
        check_vma=False,
    )
```

```python
from functools import partial

import numpy as np
import jax
import jax.numpy as jnp
from jax import lax
from jax.experimental import pallas as pl
from jax.experimental.pallas import tpu as pltpu
from jax.sharding import PartitionSpec as P

D = 1024
HD = 64
HALO = 3
TX = 8
BW = 32
BH = 8
EPSILON = 1e-05
WIN = 2 * HALO + 1
TOK = BH * BW
LANES = 128
X = 4
YH = 2
YL = 4
CORES = 2
HIDDEN = -1e30
UNIT = 16
UNIT_STEP = (
    [(-1, 0)] * 6
    + [(1, 0)] * 6
    + [(0, -1)] * 2
    + [(0, 1)] * 2
    + [(-1, -1), (-1, 1), (1, -1), (1, 1)]
)
N_UNIT = len(UNIT_STEP)
HALO_KEYS = N_UNIT * UNIT
BAND = HALO * BW
SIDE_ROWS = HALO_KEYS - 2 * BAND
LATE_Z = 5
MESH = pl.DeviceIdType.MESH


def halo_positions():
    places = [(-HALO + j // BW, j % BW, (BH - HALO) * BW + j) for j in range(BAND)]
    places += [(BH + j // BW, j % BW, j) for j in range(BAND)]

    def side(count, rows, padded, row_at, col_at, from_row, from_col):
        out = []
        for i in range(padded):
            r, c = i // HALO, i % HALO
            out.append((row_at + r, col_at + c, (from_row + r) * BW + from_col + c) if i < count else None)
        return out

    places += side(BH * HALO, BH, 2 * UNIT, 0, -HALO, 0, BW - HALO)
    places += side(BH * HALO, BH, 2 * UNIT, 0, BW, 0, 0)
    places += side(HALO * HALO, HALO, UNIT, -HALO, -HALO, BH - HALO, BW - HALO)
    places += side(HALO * HALO, HALO, UNIT, -HALO, BW, BH - HALO, 0)
    places += side(HALO * HALO, HALO, UNIT, BH, -HALO, 0, BW - HALO)
    places += side(HALO * HALO, HALO, UNIT, BH, BW, 0, 0)
    return places


def offset_codes():
    keys = [(k // BW, k % BW) for k in range(TOK)]
    keys += [(None if place is None else place[:2]) for place in halo_positions()]
    codes = np.full((len(keys), TOK), -1, np.int32)
    rows, cols = np.arange(TOK) // BW, np.arange(TOK) % BW
    for at, key in enumerate(keys):
        if key is None:
            continue
        i, j = key[0] - rows + HALO, key[1] - cols + HALO
        near = (i >= 0) & (i < WIN) & (j >= 0) & (j < WIN)
        codes[at] = np.where(near, i * WIN + j, -1)
    return codes


def side_picks():
    picks = np.zeros((SIDE_ROWS, TOK), np.float32)
    for at, place in enumerate(halo_positions()[2 * BAND :]):
        if place is not None:
            picks[at, place[2]] = 1.0
    return picks


def kernel(
    n_space,
    tile_map,
    pos_bias,
    tokens,
    gain,
    q_weight,
    k_weight,
    v_weight,
    out_weight,
    sum_keys,
    sum_values,
    codes_in,
    picks_in,
    out,
    gathered,
    normed,
    weights,
    out_w,
    codes,
    picks,
    bias,
    own_k,
    keys,
    values,
    values_t,
    queries,
    part_out,
    part_in,
    stat_out,
    stat_in,
    inverse,
    inverse_s,
    pack,
    routed,
    staged,
    halo,
    terms,
    pair_in,
    pair_sum,
    line_in,
    load_sem,
    inverse_sem,
    entered,
    tok_send,
    tok_recv,
    k_send,
    k_recv,
    v_send,
    v_recv,
    q_send,
    q_recv,
    part_send,
    part_recv,
    stat_send,
    stat_recv,
    rim_send,
    rim_recv,
    halo_send,
    halo_recv,
    pair_send,
    pair_recv,
    line_send,
    line_recv,
):
    slots = routed.shape[0]
    hub = n_space - 1
    share = keys.shape[1]
    ty = n_space // TX
    me = lax.axis_index("space")
    my_summ = lax.axis_index("summ")
    y_lo, core = my_summ // CORES, my_summ % CORES
    x_at = me % X
    y_hi = (me // X) % YH
    z_at = me // (X * YH)
    y_at = y_hi * YL + y_lo
    sibling = y_lo * CORES + 1 - core

    def local(src, dst, sem):
        return pltpu.make_async_copy(src, dst, sem)

    def remote(src, dst, send, recv, space, summ):
        return pltpu.make_async_remote_copy(
            src_ref=src,
            dst_ref=dst,
            send_sem=send,
            recv_sem=recv,
            device_id=(space, summ),
            device_id_type=MESH,
        )

    def ring(step, to_core):
        y = (y_at + step + YH * YL) % (YH * YL)
        return (z_at * YH + y // YL) * X + x_at, (y % YL) * CORES + to_core

    def line(step):
        return (y_lo + step) % YL

    barrier = pltpu.get_barrier_semaphore()

    def greet(space, summ):
        pl.semaphore_signal(barrier, inc=1, device_id=(space, summ), device_id_type=MESH)

    greet(me, sibling)
    for step in range(1, YL):
        greet(me, line(step) * CORES + core)
    for step in (1, -1, 2, -2):
        for to_core in range(CORES):
            greet(*ring(step, to_core))

    for step in range(1, X):
        greet(me - x_at + (x_at + step) % X, my_summ)

    @pl.when(me != hub)
    def _():
        greet(hub, my_summ)

    loads = [
        local(codes_in, codes, load_sem.at[0]),
        local(k_weight, weights.at[:, LANES : 2 * LANES], load_sem.at[1]),
        local(v_weight, weights.at[:, 2 * LANES : 3 * LANES], load_sem.at[2]),
        local(q_weight, weights.at[:, 0:LANES], load_sem.at[3]),
        local(picks_in, picks, load_sem.at[4]),
        local(out_weight, out_w, load_sem.at[5]),
    ]
    own_tokens = local(tokens, gathered.at[my_summ], tok_recv.at[my_summ])
    own_tokens.start()
    for load in loads:
        load.start()
    my_rows = pl.ds(pl.multiple_of(x_at * share, share), share)
    my_cols = pl.ds(pl.multiple_of(my_summ * LANES, LANES), LANES)
    local(sum_keys.at[my_rows, my_cols], keys.at[my_summ], k_recv).start()
    local(sum_values.at[my_rows, my_cols], values.at[my_summ], v_recv).start()

    to_scalars = local(inverse, inverse_s, inverse_sem)

    def prepare():
        lane = lax.broadcasted_iota(jnp.int32, inverse.shape, 1)

        def place(at, so_far):
            return so_far + jnp.where(lane == tile_map[at], at, 0)

        inverse[...] = lax.fori_loop(0, n_space, place, jnp.zeros(inverse.shape, jnp.int32))
        to_scalars.start()

        loads[0].wait()

        def fill(at, carry):
            rows = pl.ds(pl.multiple_of(at * UNIT, UNIT), UNIT)
            code = codes[rows, :]
            first = jnp.full(code.shape, HIDDEN, jnp.float32)
            second = first
            for i in range(WIN):
                for j in range(WIN):
                    here = code == i * WIN + j
                    first = jnp.where(here, pos_bias[i, 0, j], first)
                    second = jnp.where(here, pos_bias[i, 1, j], second)
            bias[0, rows, :] = first
            bias[1, rows, :] = second
            return carry

        lax.fori_loop(0, bias.shape[1] // UNIT, fill, 0)
        my_tile = tile_map[me]
        tile_row, tile_col = my_tile // TX, my_tile % TX
        edge = {
            (-1, 0): jnp.where(tile_row > 0, 0.0, HIDDEN),
            (1, 0): jnp.where(tile_row < ty - 1, 0.0, HIDDEN),
            (0, -1): jnp.where(tile_col > 0, 0.0, HIDDEN),
            (0, 1): jnp.where(tile_col < TX - 1, 0.0, HIDDEN),
        }
        for down in (-1, 1):
            for across in (-1, 1):
                edge[down, across] = jnp.minimum(edge[down, 0], edge[0, across])
        for step, hidden in edge.items():
            at = TOK + UNIT_STEP.index(step) * UNIT
            rows = slice(at, at + UNIT_STEP.count(step) * UNIT)
            for h in range(2):
                bias[h, rows, :] = bias[h, rows, :] + hidden

    @pl.when(z_at < LATE_Z)
    def _():
        prepare()

    near = 1 + (YL - 1) + 4 * CORES + (X - 1)
    pl.semaphore_wait(barrier, near + jnp.where(me == hub, n_space - 1, 0))

    @pl.when(me == hub)
    def _():
        def tell(step, carry):
            pl.semaphore_signal(
                entered,
                inc=1,
                device_id=((me + step) % n_space, my_summ),
                device_id_type=MESH,
            )
            return carry

        lax.fori_loop(1, n_space, tell, 0)

    sends = []
    for at, step in enumerate((2, 1, 3)):
        sends.append(
            remote(
                tokens,
                gathered.at[my_summ],
                tok_send.at[at],
                tok_recv.at[my_summ],
                me,
                line(step) * CORES + core,
            )
        )
    sends.append(
        remote(tokens, gathered.at[my_summ], tok_send.at[3], tok_recv.at[my_summ], me, sibling)
    )
    for send in sends:
        send.start()

    def give(source, held, send_sem, recv_sem, space, summ):
        cols = pl.ds(pl.multiple_of(summ * LANES, LANES), LANES)
        remote(source.at[my_rows, cols], held.at[my_summ], send_sem, recv_sem, space, summ).start()

    def give_summary():
        for step in (1, -1):
            for to_core in range(CORES):
                give(sum_keys, keys, k_send, k_recv, *ring(step, to_core))
        for to_core in range(CORES):
            give(sum_keys, keys, k_send, k_recv, *ring(2, to_core))
        give(sum_keys, keys, k_send, k_recv, me, sibling)
        for step in (1, -1):
            for to_core in range(CORES):
                give(sum_values, values, v_send, v_recv, *ring(step, to_core))
        for to_core in range(CORES):
            give(sum_values, values, v_send, v_recv, *ring(-2, to_core))
        give(sum_values, values, v_send, v_recv, me, sibling)

    @pl.when(z_at < LATE_Z)
    def _():
        give_summary()

    forwards = []
    for at, step in enumerate((1, 3, 2)):
        slab = line(step) * CORES + core
        local(gathered.at[slab], gathered.at[slab], tok_recv.at[slab]).wait()
        forward = remote(
            gathered.at[slab],
            gathered.at[slab],
            tok_send.at[4 + at],
            tok_recv.at[slab],
            me,
            sibling,
        )
        forward.start()
        forwards.append(forward)
    own_tokens.wait()
    for step in range(YL):
        slab = line(step) * CORES + 1 - core
        local(gathered.at[slab], gathered.at[slab], tok_recv.at[slab]).wait()

    squares = jnp.zeros((TOK, LANES), jnp.float32)
    for slab in range(YL * CORES):
        floats = gathered[slab].astype(jnp.float32)
        squares = squares + floats * floats
    scale = lax.rsqrt(jnp.sum(squares, axis=-1, keepdims=True) * (1.0 / D) + EPSILON)
    for slab in range(YL * CORES):
        cols = slice(slab * LANES, (slab + 1) * LANES)
        floats = gathered[slab].astype(jnp.float32)
        normed[:, cols] = (floats * scale * gain[:, cols]).astype(jnp.bfloat16)
    for load in loads[1:3]:
        load.wait()
    own_kv = jnp.dot(normed[...], weights[:, LANES:], preferred_element_type=jnp.float32)
    own_kv = own_kv.astype(jnp.bfloat16)
    own_k[...] = own_kv[:, :LANES]
    own_v = own_kv[:, LANES:]

    loads[4].wait()
    sides = jnp.dot(picks[...].astype(jnp.bfloat16), own_kv, preferred_element_type=jnp.float32)
    sides = sides.astype(jnp.bfloat16)
    for which in range(2):
        own = own_kv[:, which * LANES : (which + 1) * LANES]
        first = which * N_UNIT
        bands = BAND // UNIT
        pack[first : first + bands] = own[TOK - BAND :].reshape(bands, UNIT, LANES)
        pack[first + bands : first + 2 * bands] = own[:BAND].reshape(bands, UNIT, LANES)
        pack[first + 2 * bands : first + N_UNIT] = sides[
            :, which * LANES : (which + 1) * LANES
        ].reshape(N_UNIT - 2 * bands, UNIT, LANES)

    def send_rim(unit, carry):
        router = unit % n_space
        slot = unit // n_space

        @pl.when(router != me)
        def _():
            remote(
                pack.at[unit],
                routed.at[slot, me],
                rim_send,
                rim_recv.at[slot],
                router,
                my_summ,
            ).start()

        @pl.when(router == me)
        def _():
            local(pack.at[unit], routed.at[slot, me], rim_recv.at[slot]).start()

        return carry

    @pl.when(me != hub)
    def _():
        pl.semaphore_wait(entered, 1)

    lax.fori_loop(0, 2 * N_UNIT, send_rim, 0)

    loads[3].wait()
    own_q = jnp.dot(normed[...], weights[:, :LANES], preferred_element_type=jnp.float32)
    scaled = own_q.astype(jnp.bfloat16).astype(jnp.float32) * HD ** (-0.5)
    queries[x_at] = scaled.T.astype(jnp.bfloat16)
    peers = [(x_at + step) % X for step in range(X)]
    for step in range(1, X):
        remote(
            queries.at[x_at],
            queries.at[x_at],
            q_send,
            q_recv.at[x_at],
            me - x_at + peers[step],
            my_summ,
        ).start()

    def one_head(both, h):
        blank = jnp.zeros((HD, TOK), jnp.bfloat16)
        own = both[h * HD : (h + 1) * HD]
        return jnp.concatenate([own, blank] if h == 0 else [blank, own], axis=0)

    def attend(scores, v_rows):
        top = jnp.max(scores, axis=0, keepdims=True)
        weight = jnp.exp(scores - top)
        total = jnp.sum(weight, axis=0, keepdims=True)
        summed = jnp.dot(v_rows, weight.astype(jnp.bfloat16), preferred_element_type=jnp.float32)
        return top, total, summed

    @pl.when(z_at >= LATE_Z)
    def _():
        prepare()

    my_queries = queries[x_at]
    own_vt = own_v.astype(jnp.float32).T.astype(jnp.bfloat16)
    parts = [[], []]
    for h in range(2):
        scores = jnp.dot(own_k[...], one_head(my_queries, h), preferred_element_type=jnp.float32)
        parts[h].append(attend(scores + bias[h, :TOK], own_vt[h * HD : (h + 1) * HD]))

    to_scalars.wait()

    def route():
        for slot in range(slots):
            unit = me + slot * n_space

            @pl.when(unit < 2 * N_UNIT)
            def _():
                local(routed.at[slot], routed.at[slot], rim_recv.at[slot]).wait()
                kind = unit % N_UNIT
                down = jnp.where(
                    kind < 6, -1, jnp.where(kind < 12, 1, jnp.where(kind < 16, 0, jnp.where(kind < 18, -1, 1)))
                )
                across = jnp.where(
                    kind < 12,
                    0,
                    jnp.where(kind < 14, -1, jnp.where(kind < 16, 1, jnp.where(kind % 2 == 0, -1, 1))),
                )

                def pass_on(to, carry):
                    tile = tile_map[to]
                    row = jnp.clip(tile // TX + down, 0, ty - 1)
                    col = jnp.clip(tile % TX + across, 0, TX - 1)
                    holder = jnp.clip(inverse_s[0, row * TX + col], 0, n_space - 1)
                    staged[slot, to] = routed[slot, holder]

                    @pl.when(to != me)
                    def _():
                        remote(
                            staged.at[slot, to], halo.at[unit], halo_send, halo_recv, to, my_summ
                        ).start()

                    @pl.when(to == me)
                    def _():
                        local(staged.at[slot, to], halo.at[unit], halo_recv).start()

                    return carry

                lax.fori_loop(0, n_space, pass_on, 0)

    @pl.when(z_at >= LATE_Z)
    def _():
        give_summary()

    local(values, values, v_recv).wait()
    for slab in range(YL * CORES):
        values_t[:, slab * share : (slab + 1) * share] = (
            values[slab].astype(jnp.float32).T.astype(jnp.bfloat16)
        )
    local(keys, keys, k_recv).wait()

    def summary(step, carry):
        peer = (x_at + step) % X

        @pl.when(step > 0)
        def _():
            local(queries.at[peer], queries.at[peer], q_recv.at[peer]).wait()

        theirs = queries[peer]
        key_rows = keys[...].reshape(YL * CORES * share, LANES)
        tops, totals, sums = [], [], []
        for h in range(2):
            scores = jnp.dot(key_rows, one_head(theirs, h), preferred_element_type=jnp.float32)
            top, total, summed = attend(scores, values_t[h * HD : (h + 1) * HD, :])
            tops.append(top)
            totals.append(total)
            sums.append(summed)
        part_out[peer] = jnp.concatenate(sums, axis=0).astype(jnp.bfloat16)
        stat_out[peer] = jnp.concatenate(tops + totals + [jnp.zeros((4, TOK), jnp.float32)], axis=0)

        @pl.when(step > 0)
        def _():
            to = me - x_at + peer
            remote(
                part_out.at[peer], part_in.at[x_at], part_send, part_recv.at[x_at], to, my_summ
            ).start()
            remote(
                stat_out.at[peer], stat_in.at[x_at], stat_send, stat_recv.at[x_at], to, my_summ
            ).start()

        return carry

    before = jnp.clip(X - (z_at + 1) // 2 - 2 * y_hi, 0, X)
    lax.fori_loop(0, before, summary, 0)
    route()
    lax.fori_loop(before, X, summary, 0)

    local(halo, halo, halo_recv).wait()
    halo_k = halo[:N_UNIT].reshape(HALO_KEYS, LANES)
    halo_vt = halo[N_UNIT:].reshape(HALO_KEYS, LANES).astype(jnp.float32).T.astype(jnp.bfloat16)
    for h in range(2):
        scores = jnp.dot(halo_k, one_head(my_queries, h), preferred_element_type=jnp.float32)
        parts[h].append(attend(scores + bias[h, TOK:], halo_vt[h * HD : (h + 1) * HD]))

    for step in range(X):
        peer = peers[step]
        if step > 0:
            local(part_in.at[peer], part_in.at[peer], part_recv.at[peer]).wait()
            local(stat_in.at[peer], stat_in.at[peer], stat_recv.at[peer]).wait()
            rows, stats = part_in[peer], stat_in[peer]
        else:
            rows, stats = part_out[peer], stat_out[peer]
        for h in range(2):
            parts[h].append(
                (
                    stats[h : h + 1],
                    stats[2 + h : 3 + h],
                    rows[h * HD : (h + 1) * HD].astype(jnp.float32),
                )
            )
    heads = []
    for h in range(2):
        joint = parts[h][0][0]
        for top, _, _ in parts[h][1:]:
            joint = jnp.maximum(joint, top)
        total = jnp.zeros((1, TOK), jnp.float32)
        summed = jnp.zeros((HD, TOK), jnp.float32)
        for top, part_total, part_sum in parts[h]:
            factor = jnp.exp(top - joint)
            total = total + part_total * factor
            summed = summed + part_sum * factor
        heads.append(summed / total)
    attended = jnp.concatenate(heads, axis=0).T.astype(jnp.bfloat16)

    loads[5].wait()
    mixed = jnp.dot(attended, out_w[...], preferred_element_type=jnp.float32).astype(jnp.bfloat16)
    for at in range(YL):
        for side in range(CORES):
            slab = at * CORES + side
            terms[side, at] = mixed[:, slab * LANES : (slab + 1) * LANES]
    order = [line(step) for step in (2, 1, 3, 0)]
    pair = []
    for at in order:
        pair.append(
            remote(
                terms.at[1 - core, at], pair_in.at[at], pair_send.at[at], pair_recv.at[at], me, sibling
            )
        )
        pair[-1].start()
    along = []
    for at in order[:3]:
        local(pair_in.at[at], pair_in.at[at], pair_recv.at[at]).wait()
        both = terms[core, at].astype(jnp.float32) + pair_in[at].astype(jnp.float32)
        pair_sum[at] = both.astype(jnp.bfloat16)
        along.append(
            remote(
                pair_sum.at[at],
                line_in.at[y_lo],
                line_send.at[at],
                line_recv.at[y_lo],
                me,
                at * CORES + core,
            )
        )
        along[-1].start()
    local(pair_in.at[y_lo], pair_in.at[y_lo], pair_recv.at[y_lo]).wait()
    result = terms[core, y_lo].astype(jnp.float32) + pair_in[y_lo].astype(jnp.float32)
    for step in (1, 3, 2):
        at = line(step)
        local(line_in.at[at], line_in.at[at], line_recv.at[at]).wait()
        result = result + line_in[at].astype(jnp.float32)
    out[...] = result.astype(jnp.bfloat16)

    for send in sends + forwards + pair + along:
        send.wait_send()
    for sem, held in ((k_send, keys), (v_send, values)):
        sent = held.at[: YL * CORES - 1]
        local(sent, sent, sem).wait()
    for sem, held in ((q_send, queries), (part_send, part_out), (stat_send, stat_out)):
        sent = held.at[: X - 1]
        local(sent, sent, sem).wait()
    routers = [unit % n_space for unit in range(2 * N_UNIT)]
    own_units = jnp.where(me < (2 * N_UNIT) % n_space, 1, 0) + 2 * N_UNIT // n_space
    for count in sorted({routers.count(at) for at in range(n_space)}):

        @pl.when(own_units == count)
        def _():
            sent = pack.at[: 2 * N_UNIT - count]
            local(sent, sent, rim_send).wait()

    for slot in range(slots):

        @pl.when(me + slot * n_space < 2 * N_UNIT)
        def _():
            sent = staged.at[slot, : n_space - 1]
            local(sent, sent, halo_send).wait()


def shards(
    n_space,
    tokens,
    tile_map,
    norm_gain,
    q_weight,
    k_weight,
    v_weight,
    out_weight,
    pos_bias,
    sum_keys,
    sum_values,
):
    share = sum_keys.shape[0] // X
    slots = -(-2 * N_UNIT // n_space)
    bf16 = jnp.bfloat16
    f32 = jnp.float32
    dma = pltpu.SemaphoreType.DMA
    anywhere = pl.BlockSpec(memory_space=pl.ANY)
    scalars = pl.BlockSpec(memory_space=pltpu.SMEM)
    vector = pl.BlockSpec(memory_space=pltpu.VMEM)
    slab = (TOK, LANES)
    turned = (LANES, TOK)
    scratch = [
        pltpu.VMEM((YL * CORES,) + slab, bf16),
        pltpu.VMEM((TOK, D), bf16),
        pltpu.VMEM((D, 3 * LANES), bf16),
        pltpu.VMEM((LANES, D), bf16),
        pltpu.VMEM((TOK + HALO_KEYS, TOK), jnp.int32),
        pltpu.VMEM((SIDE_ROWS, TOK), f32),
        pltpu.VMEM((2, TOK + HALO_KEYS, TOK), f32),
        pltpu.VMEM(slab, bf16),
        pltpu.VMEM((YL * CORES, share, LANES), bf16),
        pltpu.VMEM((YL * CORES, share, LANES), bf16),
        pltpu.VMEM((LANES, YL * CORES * share), bf16),
        pltpu.VMEM((X,) + turned, bf16),
        pltpu.VMEM((X,) + turned, bf16),
        pltpu.VMEM((X,) + turned, bf16),
        pltpu.VMEM((X, 8, TOK), f32),
        pltpu.VMEM((X, 8, TOK), f32),
        pltpu.VMEM((8, LANES), jnp.int32),
        pltpu.SMEM((8, LANES), jnp.int32),
        pltpu.VMEM((2 * N_UNIT, UNIT, LANES), bf16),
        pltpu.VMEM((slots, n_space, UNIT, LANES), bf16),
        pltpu.VMEM((slots, n_space, UNIT, LANES), bf16),
        pltpu.VMEM((2 * N_UNIT, UNIT, LANES), bf16),
        pltpu.VMEM((CORES, YL) + slab, bf16),
        pltpu.VMEM((YL,) + slab, bf16),
        pltpu.VMEM((YL,) + slab, bf16),
        pltpu.VMEM((YL,) + slab, bf16),
        dma((6,)),
        dma,
        pltpu.SemaphoreType.REGULAR,
        dma((7,)),
        dma((YL * CORES,)),
        dma,
        dma,
        dma,
        dma,
        dma,
        dma((X,)),
        dma,
        dma((X,)),
        dma,
        dma((X,)),
        dma,
        dma((slots,)),
        dma,
        dma,
        dma((YL,)),
        dma((YL,)),
        dma((YL,)),
        dma((YL,)),
    ]
    mixed = pl.pallas_call(
        partial(kernel, n_space),
        out_shape=jax.ShapeDtypeStruct(slab, bf16),
        in_specs=[scalars, scalars, anywhere, vector] + [anywhere] * 8,
        out_specs=vector,
        scratch_shapes=scratch,
        compiler_params=pltpu.CompilerParams(
            collective_id=0, has_side_effects=True, vmem_limit_bytes=63 * 1024 * 1024
        ),
        name="tile_attention",
    )(
        tile_map,
        pos_bias.transpose(1, 0, 2),
        tokens.reshape(slab),
        norm_gain.reshape(1, D),
        q_weight,
        k_weight,
        v_weight,
        out_weight,
        sum_keys,
        sum_values,
        jnp.asarray(offset_codes()),
        jnp.asarray(side_picks()),
    )
    return mixed.reshape(1, BH, BW, LANES)


def solution(mesh):
    return jax.shard_map(
        partial(shards, mesh.shape["space"]),
        mesh=mesh,
        in_specs=(
            P("space", None, None, "summ"),
            P(),
            P(),
            P(None, "summ"),
            P(None, "summ"),
            P(None, "summ"),
            P("summ", None),
            P("summ", None, None),
            P("summ", None),
            P("summ", None),
        ),
        out_specs=P("space", None, None, "summ"),
        check_vma=False,
    )
```

```python
from functools import partial

import numpy as np
import jax
import jax.numpy as jnp
from jax import lax
from jax.experimental import pallas as pl
from jax.experimental.pallas import tpu as pltpu
from jax.sharding import PartitionSpec as P

D = 1024
HD = 64
HALO = 3
TX = 8
BW = 32
BH = 8
EPSILON = 1e-05
WIN = 2 * HALO + 1
TOK = BH * BW
LANES = 128
X = 4
YH = 2
YL = 4
CORES = 2
HIDDEN = -1e30
UNIT = 16
UNIT_STEP = (
    [(-1, 0)] * 6
    + [(1, 0)] * 6
    + [(0, -1)] * 2
    + [(0, 1)] * 2
    + [(-1, -1), (-1, 1), (1, -1), (1, 1)]
)
N_UNIT = len(UNIT_STEP)
HALO_KEYS = N_UNIT * UNIT
BAND = HALO * BW
SIDE_ROWS = HALO_KEYS - 2 * BAND
LATE_Z = 5
MESH = pl.DeviceIdType.MESH


def halo_positions():
    places = [(-HALO + j // BW, j % BW, (BH - HALO) * BW + j) for j in range(BAND)]
    places += [(BH + j // BW, j % BW, j) for j in range(BAND)]

    def side(count, rows, padded, row_at, col_at, from_row, from_col):
        out = []
        for i in range(padded):
            r, c = i // HALO, i % HALO
            out.append((row_at + r, col_at + c, (from_row + r) * BW + from_col + c) if i < count else None)
        return out

    places += side(BH * HALO, BH, 2 * UNIT, 0, -HALO, 0, BW - HALO)
    places += side(BH * HALO, BH, 2 * UNIT, 0, BW, 0, 0)
    places += side(HALO * HALO, HALO, UNIT, -HALO, -HALO, BH - HALO, BW - HALO)
    places += side(HALO * HALO, HALO, UNIT, -HALO, BW, BH - HALO, 0)
    places += side(HALO * HALO, HALO, UNIT, BH, -HALO, 0, BW - HALO)
    places += side(HALO * HALO, HALO, UNIT, BH, BW, 0, 0)
    return places


def offset_codes():
    keys = [(k // BW, k % BW) for k in range(TOK)]
    keys += [(None if place is None else place[:2]) for place in halo_positions()]
    codes = np.full((len(keys), TOK), -1, np.int32)
    rows, cols = np.arange(TOK) // BW, np.arange(TOK) % BW
    for at, key in enumerate(keys):
        if key is None:
            continue
        i, j = key[0] - rows + HALO, key[1] - cols + HALO
        near = (i >= 0) & (i < WIN) & (j >= 0) & (j < WIN)
        codes[at] = np.where(near, i * WIN + j, -1)
    return codes


def side_picks():
    picks = np.zeros((SIDE_ROWS, TOK), np.float32)
    for at, place in enumerate(halo_positions()[2 * BAND :]):
        if place is not None:
            picks[at, place[2]] = 1.0
    return picks


def kernel(
    n_space,
    tile_map_in,
    pos_bias_in,
    tokens,
    gain_in,
    q_weight,
    k_weight,
    v_weight,
    out_weight,
    sum_keys,
    sum_values,
    codes_in,
    picks_in,
    out,
    tile_map,
    pos_bias,
    gain,
    gathered,
    normed,
    weights,
    out_w,
    codes,
    picks,
    bias,
    own_kv,
    keys,
    values,
    values_t,
    queries,
    part_out,
    part_in,
    stat_out,
    stat_in,
    inverse,
    inverse_s,
    pack,
    routed,
    staged,
    halo,
    terms,
    pair_in,
    pair_sum,
    line_in,
    load_sem,
    inverse_sem,
    entered,
    tok_send,
    tok_recv,
    k_send,
    k_recv,
    v_send,
    v_recv,
    q_send,
    q_recv,
    part_send,
    part_recv,
    stat_send,
    stat_recv,
    rim_send,
    rim_recv,
    halo_send,
    halo_recv,
    pair_send,
    pair_recv,
    line_send,
    line_recv,
):
    slots = routed.shape[0]
    hub = n_space - 1
    share = keys.shape[1]
    ty = n_space // TX
    me = lax.axis_index("space")
    my_summ = lax.axis_index("summ")
    y_lo, core = my_summ // CORES, my_summ % CORES
    x_at = me % X
    y_hi = (me // X) % YH
    z_at = me // (X * YH)
    y_at = y_hi * YL + y_lo
    sibling = y_lo * CORES + 1 - core

    def local(src, dst, sem):
        return pltpu.make_async_copy(src, dst, sem)

    def remote(src, dst, send, recv, space, summ):
        return pltpu.make_async_remote_copy(
            src_ref=src,
            dst_ref=dst,
            send_sem=send,
            recv_sem=recv,
            device_id=(space, summ),
            device_id_type=MESH,
        )

    def ring(step, to_core):
        y = (y_at + step + YH * YL) % (YH * YL)
        return (z_at * YH + y // YL) * X + x_at, (y % YL) * CORES + to_core

    def line(step):
        return (y_lo + step) % YL

    barrier = pltpu.get_barrier_semaphore()

    def greet(space, summ):
        pl.semaphore_signal(barrier, inc=1, device_id=(space, summ), device_id_type=MESH)

    greet(me, sibling)
    for step in range(1, YL):
        greet(me, line(step) * CORES + core)
    for step in (1, -1, 2, -2):
        for to_core in range(CORES):
            greet(*ring(step, to_core))

    for step in range(1, X):
        greet(me - x_at + (x_at + step) % X, my_summ)

    @pl.when(me != hub)
    def _():
        greet(hub, my_summ)

    loads = [
        local(codes_in, codes, load_sem.at[0]),
        local(k_weight, weights.at[:, LANES : 2 * LANES], load_sem.at[1]),
        local(v_weight, weights.at[:, 2 * LANES : 3 * LANES], load_sem.at[2]),
        local(q_weight, weights.at[:, 0:LANES], load_sem.at[3]),
        local(picks_in, picks, load_sem.at[4]),
        local(out_weight, out_w, load_sem.at[5]),
        local(gain_in, gain, load_sem.at[6]),
        local(tile_map_in, tile_map, load_sem.at[7]),
        local(pos_bias_in, pos_bias, load_sem.at[8]),
    ]
    half_rows = [pl.ds(half * (TOK // 2), TOK // 2) for half in range(2)]
    own_tokens = [
        local(tokens.at[rows], gathered.at[my_summ, rows], tok_recv.at[half, my_summ])
        for half, rows in enumerate(half_rows)
    ]
    for load in own_tokens:
        load.start()
    for load in loads:
        load.start()
    my_rows = pl.ds(pl.multiple_of(x_at * share, share), share)
    my_cols = pl.ds(pl.multiple_of(my_summ * LANES, LANES), LANES)
    local(sum_keys.at[my_rows, my_cols], keys.at[my_summ], k_recv).start()
    local(sum_values.at[my_rows, my_cols], values.at[my_summ], v_recv).start()

    to_scalars = local(inverse, inverse_s, inverse_sem)

    def prepare():
        loads[7].wait()
        lane = lax.broadcasted_iota(jnp.int32, inverse.shape, 1)

        def place(at, so_far):
            return so_far + jnp.where(lane == tile_map[at], at, 0)

        inverse[...] = lax.fori_loop(0, n_space, place, jnp.zeros(inverse.shape, jnp.int32))
        to_scalars.start()

        loads[0].wait()
        loads[8].wait()

        def fill(at, carry):
            rows = pl.ds(pl.multiple_of(at * UNIT, UNIT), UNIT)
            code = codes[rows, :]
            first = jnp.full(code.shape, HIDDEN, jnp.float32)
            second = first
            for i in range(WIN):
                for j in range(WIN):
                    here = code == i * WIN + j
                    first = jnp.where(here, pos_bias[i, 0, j], first)
                    second = jnp.where(here, pos_bias[i, 1, j], second)
            bias[0, rows, :] = first
            bias[1, rows, :] = second
            return carry

        lax.fori_loop(0, bias.shape[1] // UNIT, fill, 0)
        my_tile = tile_map[me]
        tile_row, tile_col = my_tile // TX, my_tile % TX
        edge = {
            (-1, 0): jnp.where(tile_row > 0, 0.0, HIDDEN),
            (1, 0): jnp.where(tile_row < ty - 1, 0.0, HIDDEN),
            (0, -1): jnp.where(tile_col > 0, 0.0, HIDDEN),
            (0, 1): jnp.where(tile_col < TX - 1, 0.0, HIDDEN),
        }
        for down in (-1, 1):
            for across in (-1, 1):
                edge[down, across] = jnp.minimum(edge[down, 0], edge[0, across])
        for step, hidden in edge.items():
            at = TOK + UNIT_STEP.index(step) * UNIT
            rows = slice(at, at + UNIT_STEP.count(step) * UNIT)
            for h in range(2):
                bias[h, rows, :] = bias[h, rows, :] + hidden

    @pl.when(z_at < LATE_Z)
    def _():
        prepare()

    near = 1 + (YL - 1) + 4 * CORES + (X - 1)
    pl.semaphore_wait(barrier, near + jnp.where(me == hub, n_space - 1, 0))

    @pl.when(me == hub)
    def _():
        def tell(step, carry):
            pl.semaphore_signal(
                entered,
                inc=1,
                device_id=((me + step) % n_space, my_summ),
                device_id_type=MESH,
            )
            return carry

        lax.fori_loop(1, n_space, tell, 0)

    sends = []

    def send_slab(source, slab, half, summ):
        at = gathered.at[slab, half_rows[half]]
        sends.append(
            remote(
                source, at, tok_send.at[len(sends)], tok_recv.at[half, slab], me, summ
            )
        )
        sends[-1].start()

    for half in range(2):
        for step in (2, 1, 3):
            send_slab(tokens.at[half_rows[half]], my_summ, half, line(step) * CORES + core)
        send_slab(tokens.at[half_rows[half]], my_summ, half, sibling)

    def give(source, held, send_sem, recv_sem, space, summ):
        cols = pl.ds(pl.multiple_of(summ * LANES, LANES), LANES)
        remote(source.at[my_rows, cols], held.at[my_summ], send_sem, recv_sem, space, summ).start()

    def give_summary():
        for step in (1, -1):
            for to_core in range(CORES):
                give(sum_keys, keys, k_send, k_recv, *ring(step, to_core))
        for to_core in range(CORES):
            give(sum_keys, keys, k_send, k_recv, *ring(2, to_core))
        give(sum_keys, keys, k_send, k_recv, me, sibling)
        for step in (1, -1):
            for to_core in range(CORES):
                give(sum_values, values, v_send, v_recv, *ring(step, to_core))
        for to_core in range(CORES):
            give(sum_values, values, v_send, v_recv, *ring(-2, to_core))
        give(sum_values, values, v_send, v_recv, me, sibling)

    @pl.when(z_at < LATE_Z)
    def _():
        give_summary()

    def await_slab(slab, half):
        held = gathered.at[slab, half_rows[half]]
        local(held, held, tok_recv.at[half, slab]).wait()

    def await_half(half):
        for step in (1, 3, 2):
            slab = line(step) * CORES + core
            await_slab(slab, half)
            send_slab(gathered.at[slab, half_rows[half]], slab, half, sibling)
        own_tokens[half].wait()
        for step in range(YL):
            await_slab(line(step) * CORES + 1 - core, half)

    def project_half(half):
        rows = half_rows[half]
        squares = jnp.zeros((TOK // 2, LANES), jnp.float32)
        for slab in range(YL * CORES):
            floats = gathered[slab, rows, :].astype(jnp.float32)
            squares = squares + floats * floats
        scale = lax.rsqrt(jnp.sum(squares, axis=-1, keepdims=True) * (1.0 / D) + EPSILON)
        for slab in range(YL * CORES):
            cols = slice(slab * LANES, (slab + 1) * LANES)
            floats = gathered[slab, rows, :].astype(jnp.float32)
            normed[rows, cols] = (floats * scale * gain[:, cols]).astype(jnp.bfloat16)
        result = jnp.dot(normed[rows, :], weights[:, LANES:], preferred_element_type=jnp.float32)
        own_kv[rows, :] = result.astype(jnp.bfloat16)

    bands = BAND // UNIT

    def send_rim(unit, carry):
        router = unit % n_space
        slot = unit // n_space

        @pl.when(router != me)
        def _():
            remote(
                pack.at[unit],
                routed.at[slot, me],
                rim_send,
                rim_recv.at[slot],
                router,
                my_summ,
            ).start()

        @pl.when(router == me)
        def _():
            local(pack.at[unit], routed.at[slot, me], rim_recv.at[slot]).start()

        return carry

    await_half(0)
    loads[6].wait()
    for load in loads[1:3]:
        load.wait()
    project_half(0)

    @pl.when(me != hub)
    def _():
        pl.semaphore_wait(entered, 1)

    for which in range(2):
        cols = slice(which * LANES, (which + 1) * LANES)
        first = which * N_UNIT + bands
        pack[first : first + bands] = own_kv[:BAND, cols].reshape(bands, UNIT, LANES)
        lax.fori_loop(first, first + bands, send_rim, 0)
    await_half(1)
    project_half(1)
    loads[4].wait()
    sides = jnp.dot(
        picks[...].astype(jnp.bfloat16), own_kv[...], preferred_element_type=jnp.float32
    )
    sides = sides.astype(jnp.bfloat16)
    for which in range(2):
        cols = slice(which * LANES, (which + 1) * LANES)
        first = which * N_UNIT
        pack[first : first + bands] = own_kv[TOK - BAND :, cols].reshape(bands, UNIT, LANES)
        pack[first + 2 * bands : first + N_UNIT] = sides[:, cols].reshape(
            N_UNIT - 2 * bands, UNIT, LANES
        )
        lax.fori_loop(first, first + bands, send_rim, 0)
        lax.fori_loop(first + 2 * bands, first + N_UNIT, send_rim, 0)
    own_k = own_kv[:, :LANES]
    own_v = own_kv[:, LANES:]

    loads[3].wait()
    own_q = jnp.dot(normed[...], weights[:, :LANES], preferred_element_type=jnp.float32)
    scaled = own_q.astype(jnp.bfloat16).astype(jnp.float32) * HD ** (-0.5)
    queries[x_at] = scaled.T.astype(jnp.bfloat16)
    peers = [(x_at + step) % X for step in range(X)]
    def one_head(both, h):
        blank = jnp.zeros((HD, TOK), jnp.bfloat16)
        own = both[h * HD : (h + 1) * HD]
        return jnp.concatenate([own, blank] if h == 0 else [blank, own], axis=0)

    def attend(scores, v_rows):
        top = jnp.max(scores, axis=0, keepdims=True)
        weight = jnp.exp(scores - top)
        total = jnp.sum(weight, axis=0, keepdims=True)
        summed = jnp.dot(v_rows, weight.astype(jnp.bfloat16), preferred_element_type=jnp.float32)
        return top, total, summed

    @pl.when(z_at >= LATE_Z)
    def _():
        prepare()

    my_queries = queries[x_at]
    own_vt = own_v.astype(jnp.float32).T.astype(jnp.bfloat16)
    parts = [[], []]
    for h in range(2):
        scores = jnp.dot(own_k, one_head(my_queries, h), preferred_element_type=jnp.float32)
        parts[h].append(attend(scores + bias[h, :TOK], own_vt[h * HD : (h + 1) * HD]))

    for step in range(1, X):
        remote(
            queries.at[x_at],
            queries.at[x_at],
            q_send,
            q_recv.at[x_at],
            me - x_at + peers[step],
            my_summ,
        ).start()

    to_scalars.wait()

    def route():
        for slot in range(slots):
            unit = me + slot * n_space

            @pl.when(unit < 2 * N_UNIT)
            def _():
                local(routed.at[slot], routed.at[slot], rim_recv.at[slot]).wait()
                kind = unit % N_UNIT
                down = jnp.where(
                    kind < 6, -1, jnp.where(kind < 12, 1, jnp.where(kind < 16, 0, jnp.where(kind < 18, -1, 1)))
                )
                across = jnp.where(
                    kind < 12,
                    0,
                    jnp.where(kind < 14, -1, jnp.where(kind < 16, 1, jnp.where(kind % 2 == 0, -1, 1))),
                )

                def pass_on(at, carry):
                    to = at // 8 * 8 + (at + me) % 8
                    tile = tile_map[to]
                    row = jnp.clip(tile // TX + down, 0, ty - 1)
                    col = jnp.clip(tile % TX + across, 0, TX - 1)
                    holder = jnp.clip(inverse_s[0, row * TX + col], 0, n_space - 1)
                    staged[slot, to] = routed[slot, holder]

                    @pl.when(to != me)
                    def _():
                        remote(
                            staged.at[slot, to], halo.at[unit], halo_send, halo_recv, to, my_summ
                        ).start()

                    @pl.when(to == me)
                    def _():
                        local(staged.at[slot, to], halo.at[unit], halo_recv).start()

                    return carry

                lax.fori_loop(0, n_space, pass_on, 0)

    @pl.when(z_at >= LATE_Z)
    def _():
        give_summary()

    before = jnp.where(y_hi == 0, jnp.clip(X - z_at, 0, X), jnp.where(z_at == 0, 2, 0))

    @pl.when(before == 0)
    def _():
        route()

    local(values, values, v_recv).wait()
    for slab in range(YL * CORES):
        values_t[:, slab * share : (slab + 1) * share] = (
            values[slab].astype(jnp.float32).T.astype(jnp.bfloat16)
        )
    local(keys, keys, k_recv).wait()

    def summary(step, carry):
        peer = (x_at + step) % X

        @pl.when(step > 0)
        def _():
            local(queries.at[peer], queries.at[peer], q_recv.at[peer]).wait()

        theirs = queries[peer]
        key_rows = keys[...].reshape(YL * CORES * share, LANES)
        tops, totals, sums = [], [], []
        for h in range(2):
            scores = jnp.dot(key_rows, one_head(theirs, h), preferred_element_type=jnp.float32)
            top, total, summed = attend(scores, values_t[h * HD : (h + 1) * HD, :])
            tops.append(top)
            totals.append(total)
            sums.append(summed)
        part_out[peer] = jnp.concatenate(sums, axis=0).astype(jnp.bfloat16)
        stat_out[peer] = jnp.concatenate(tops + totals + [jnp.zeros((4, TOK), jnp.float32)], axis=0)

        @pl.when(step > 0)
        def _():
            to = me - x_at + peer
            remote(
                part_out.at[peer], part_in.at[x_at], part_send, part_recv.at[x_at], to, my_summ
            ).start()
            remote(
                stat_out.at[peer], stat_in.at[x_at], stat_send, stat_recv.at[x_at], to, my_summ
            ).start()

        return carry

    lax.fori_loop(0, before, summary, 0)

    @pl.when(before > 0)
    def _():
        route()

    lax.fori_loop(before, X, summary, 0)

    local(halo, halo, halo_recv).wait()
    halo_k = halo[:N_UNIT].reshape(HALO_KEYS, LANES)
    halo_vt = halo[N_UNIT:].reshape(HALO_KEYS, LANES).astype(jnp.float32).T.astype(jnp.bfloat16)
    for h in range(2):
        scores = jnp.dot(halo_k, one_head(my_queries, h), preferred_element_type=jnp.float32)
        parts[h].append(attend(scores + bias[h, TOK:], halo_vt[h * HD : (h + 1) * HD]))

    for step in range(X):
        peer = peers[step]
        if step > 0:
            local(part_in.at[peer], part_in.at[peer], part_recv.at[peer]).wait()
            local(stat_in.at[peer], stat_in.at[peer], stat_recv.at[peer]).wait()
            rows, stats = part_in[peer], stat_in[peer]
        else:
            rows, stats = part_out[peer], stat_out[peer]
        for h in range(2):
            parts[h].append(
                (
                    stats[h : h + 1],
                    stats[2 + h : 3 + h],
                    rows[h * HD : (h + 1) * HD].astype(jnp.float32),
                )
            )
    heads = []
    for h in range(2):
        joint = parts[h][0][0]
        for top, _, _ in parts[h][1:]:
            joint = jnp.maximum(joint, top)
        total = jnp.zeros((1, TOK), jnp.float32)
        summed = jnp.zeros((HD, TOK), jnp.float32)
        for top, part_total, part_sum in parts[h]:
            factor = jnp.exp(top - joint)
            total = total + part_total * factor
            summed = summed + part_sum * factor
        heads.append(summed / total)
    attended = jnp.concatenate(heads, axis=0).T.astype(jnp.bfloat16)

    loads[5].wait()
    mixed = jnp.dot(attended, out_w[...], preferred_element_type=jnp.float32).astype(jnp.bfloat16)
    for at in range(YL):
        for side in range(CORES):
            slab = at * CORES + side
            terms[side, at] = mixed[:, slab * LANES : (slab + 1) * LANES]
    order = [line(step) for step in (2, 1, 3, 0)]
    pair = []
    for at in order:
        pair.append(
            remote(
                terms.at[1 - core, at], pair_in.at[at], pair_send.at[at], pair_recv.at[at], me, sibling
            )
        )
        pair[-1].start()
    along = []
    for at in order[:3]:
        local(pair_in.at[at], pair_in.at[at], pair_recv.at[at]).wait()
        both = terms[core, at].astype(jnp.float32) + pair_in[at].astype(jnp.float32)
        pair_sum[at] = both.astype(jnp.bfloat16)
        along.append(
            remote(
                pair_sum.at[at],
                line_in.at[y_lo],
                line_send.at[at],
                line_recv.at[y_lo],
                me,
                at * CORES + core,
            )
        )
        along[-1].start()
    local(pair_in.at[y_lo], pair_in.at[y_lo], pair_recv.at[y_lo]).wait()
    result = terms[core, y_lo].astype(jnp.float32) + pair_in[y_lo].astype(jnp.float32)
    for step in (1, 3, 2):
        at = line(step)
        local(line_in.at[at], line_in.at[at], line_recv.at[at]).wait()
        result = result + line_in[at].astype(jnp.float32)
    out[...] = result.astype(jnp.bfloat16)

    for send in sends + pair + along:
        send.wait_send()
    for sem, held in ((k_send, keys), (v_send, values)):
        sent = held.at[: YL * CORES - 1]
        local(sent, sent, sem).wait()
    for sem, held in ((q_send, queries), (part_send, part_out), (stat_send, stat_out)):
        sent = held.at[: X - 1]
        local(sent, sent, sem).wait()
    routers = [unit % n_space for unit in range(2 * N_UNIT)]
    own_units = jnp.where(me < (2 * N_UNIT) % n_space, 1, 0) + 2 * N_UNIT // n_space
    for count in sorted({routers.count(at) for at in range(n_space)}):

        @pl.when(own_units == count)
        def _():
            sent = pack.at[: 2 * N_UNIT - count]
            local(sent, sent, rim_send).wait()

    for slot in range(slots):

        @pl.when(me + slot * n_space < 2 * N_UNIT)
        def _():
            sent = staged.at[slot, : n_space - 1]
            local(sent, sent, halo_send).wait()


def shards(
    n_space,
    tokens,
    tile_map,
    norm_gain,
    q_weight,
    k_weight,
    v_weight,
    out_weight,
    pos_bias,
    sum_keys,
    sum_values,
):
    share = sum_keys.shape[0] // X
    slots = -(-2 * N_UNIT // n_space)
    bf16 = jnp.bfloat16
    f32 = jnp.float32
    dma = pltpu.SemaphoreType.DMA
    anywhere = pl.BlockSpec(memory_space=pl.ANY)
    vector = pl.BlockSpec(memory_space=pltpu.VMEM)
    slab = (TOK, LANES)
    turned = (LANES, TOK)
    scratch = [
        pltpu.SMEM((n_space,), jnp.int32),
        pltpu.SMEM((WIN, 2, WIN), f32),
        pltpu.VMEM((1, D), f32),
        pltpu.VMEM((YL * CORES,) + slab, bf16),
        pltpu.VMEM((TOK, D), bf16),
        pltpu.VMEM((D, 3 * LANES), bf16),
        pltpu.VMEM((LANES, D), bf16),
        pltpu.VMEM((TOK + HALO_KEYS, TOK), jnp.int32),
        pltpu.VMEM((SIDE_ROWS, TOK), f32),
        pltpu.VMEM((2, TOK + HALO_KEYS, TOK), f32),
        pltpu.VMEM((TOK, 2 * LANES), bf16),
        pltpu.VMEM((YL * CORES, share, LANES), bf16),
        pltpu.VMEM((YL * CORES, share, LANES), bf16),
        pltpu.VMEM((LANES, YL * CORES * share), bf16),
        pltpu.VMEM((X,) + turned, bf16),
        pltpu.VMEM((X,) + turned, bf16),
        pltpu.VMEM((X,) + turned, bf16),
        pltpu.VMEM((X, 8, TOK), f32),
        pltpu.VMEM((X, 8, TOK), f32),
        pltpu.VMEM((8, LANES), jnp.int32),
        pltpu.SMEM((8, LANES), jnp.int32),
        pltpu.VMEM((2 * N_UNIT, UNIT, LANES), bf16),
        pltpu.VMEM((slots, n_space, UNIT, LANES), bf16),
        pltpu.VMEM((slots, n_space, UNIT, LANES), bf16),
        pltpu.VMEM((2 * N_UNIT, UNIT, LANES), bf16),
        pltpu.VMEM((CORES, YL) + slab, bf16),
        pltpu.VMEM((YL,) + slab, bf16),
        pltpu.VMEM((YL,) + slab, bf16),
        pltpu.VMEM((YL,) + slab, bf16),
        dma((9,)),
        dma,
        pltpu.SemaphoreType.REGULAR,
        dma((14,)),
        dma((2, YL * CORES)),
        dma,
        dma,
        dma,
        dma,
        dma,
        dma((X,)),
        dma,
        dma((X,)),
        dma,
        dma((X,)),
        dma,
        dma((slots,)),
        dma,
        dma,
        dma((YL,)),
        dma((YL,)),
        dma((YL,)),
        dma((YL,)),
    ]
    mixed = pl.pallas_call(
        partial(kernel, n_space),
        out_shape=jax.ShapeDtypeStruct(slab, bf16),
        in_specs=[anywhere] * 12,
        out_specs=vector,
        scratch_shapes=scratch,
        compiler_params=pltpu.CompilerParams(
            collective_id=0, has_side_effects=True, vmem_limit_bytes=63 * 1024 * 1024
        ),
        name="tile_attention",
    )(
        tile_map,
        pos_bias.transpose(1, 0, 2),
        tokens.reshape(slab),
        norm_gain.reshape(1, D),
        q_weight,
        k_weight,
        v_weight,
        out_weight,
        sum_keys,
        sum_values,
        jnp.asarray(offset_codes()),
        jnp.asarray(side_picks()),
    )
    return mixed.reshape(1, BH, BW, LANES)


def solution(mesh):
    return jax.shard_map(
        partial(shards, mesh.shape["space"]),
        mesh=mesh,
        in_specs=(
            P("space", None, None, "summ"),
            P(),
            P(),
            P(None, "summ"),
            P(None, "summ"),
            P(None, "summ"),
            P("summ", None),
            P("summ", None, None),
            P("summ", None),
            P("summ", None),
        ),
        out_specs=P("space", None, None, "summ"),
        check_vma=False,
    )
```

```python
from functools import partial

import numpy as np
import jax
import jax.numpy as jnp
from jax import lax
from jax.experimental import pallas as pl
from jax.experimental.pallas import tpu as pltpu
from jax.sharding import PartitionSpec as P

D = 1024
HD = 64
HALO = 3
TX = 8
BW = 32
BH = 8
EPSILON = 1e-05
WIN = 2 * HALO + 1
TOK = BH * BW
LANES = 128
X = 4
YH = 2
YL = 4
CORES = 2
HIDDEN = -1e30
UNIT = 16
UNIT_STEP = (
    [(-1, 0)] * 6
    + [(1, 0)] * 6
    + [(0, -1)] * 2
    + [(0, 1)] * 2
    + [(-1, -1), (-1, 1), (1, -1), (1, 1)]
)
N_UNIT = len(UNIT_STEP)
HALO_KEYS = N_UNIT * UNIT
BAND = HALO * BW
SIDE_ROWS = HALO_KEYS - 2 * BAND
LATE_Z = 5
MESH = pl.DeviceIdType.MESH


def halo_positions():
    places = [(-HALO + j // BW, j % BW, (BH - HALO) * BW + j) for j in range(BAND)]
    places += [(BH + j // BW, j % BW, j) for j in range(BAND)]

    def side(count, rows, padded, row_at, col_at, from_row, from_col):
        out = []
        for i in range(padded):
            r, c = i // HALO, i % HALO
            out.append((row_at + r, col_at + c, (from_row + r) * BW + from_col + c) if i < count else None)
        return out

    places += side(BH * HALO, BH, 2 * UNIT, 0, -HALO, 0, BW - HALO)
    places += side(BH * HALO, BH, 2 * UNIT, 0, BW, 0, 0)
    places += side(HALO * HALO, HALO, UNIT, -HALO, -HALO, BH - HALO, BW - HALO)
    places += side(HALO * HALO, HALO, UNIT, -HALO, BW, BH - HALO, 0)
    places += side(HALO * HALO, HALO, UNIT, BH, -HALO, 0, BW - HALO)
    places += side(HALO * HALO, HALO, UNIT, BH, BW, 0, 0)
    return places


def offset_codes():
    keys = [(k // BW, k % BW) for k in range(TOK)]
    keys += [(None if place is None else place[:2]) for place in halo_positions()]
    codes = np.full((len(keys), TOK), -1, np.int32)
    rows, cols = np.arange(TOK) // BW, np.arange(TOK) % BW
    for at, key in enumerate(keys):
        if key is None:
            continue
        i, j = key[0] - rows + HALO, key[1] - cols + HALO
        near = (i >= 0) & (i < WIN) & (j >= 0) & (j < WIN)
        codes[at] = np.where(near, i * WIN + j, -1)
    return codes


def side_picks():
    picks = np.zeros((SIDE_ROWS, TOK), np.float32)
    for at, place in enumerate(halo_positions()[2 * BAND :]):
        if place is not None:
            picks[at, place[2]] = 1.0
    return picks


def kernel(
    n_space,
    tile_map_in,
    pos_bias_in,
    tokens,
    gain_in,
    q_weight,
    k_weight,
    v_weight,
    out_weight,
    sum_keys,
    sum_values,
    codes_in,
    picks_in,
    out,
    tile_map,
    pos_bias,
    gain,
    gathered,
    normed,
    weights,
    out_w,
    codes,
    picks,
    bias,
    own_kv,
    keys,
    values,
    values_t,
    queries,
    part_out,
    part_in,
    stat_out,
    stat_in,
    inverse,
    inverse_s,
    pack,
    routed,
    staged,
    halo,
    terms,
    pair_in,
    pair_sum,
    line_in,
    load_sem,
    inverse_sem,
    entered,
    tok_send,
    tok_recv,
    k_send,
    k_recv,
    v_send,
    v_recv,
    q_send,
    q_recv,
    part_send,
    part_recv,
    stat_send,
    stat_recv,
    rim_send,
    rim_recv,
    halo_send,
    halo_recv,
    pair_send,
    pair_recv,
    line_send,
    line_recv,
):
    slots = routed.shape[0]
    hub = n_space - 1
    share = keys.shape[1]
    ty = n_space // TX
    me = lax.axis_index("space")
    my_summ = lax.axis_index("summ")
    y_lo, core = my_summ // CORES, my_summ % CORES
    x_at = me % X
    y_hi = (me // X) % YH
    z_at = me // (X * YH)
    y_at = y_hi * YL + y_lo
    sibling = y_lo * CORES + 1 - core

    def local(src, dst, sem):
        return pltpu.make_async_copy(src, dst, sem)

    def remote(src, dst, send, recv, space, summ):
        return pltpu.make_async_remote_copy(
            src_ref=src,
            dst_ref=dst,
            send_sem=send,
            recv_sem=recv,
            device_id=(space, summ),
            device_id_type=MESH,
        )

    def ring(step, to_core):
        y = (y_at + step + YH * YL) % (YH * YL)
        return (z_at * YH + y // YL) * X + x_at, (y % YL) * CORES + to_core

    def line(step):
        return (y_lo + step) % YL

    barrier = pltpu.get_barrier_semaphore()

    def greet(space, summ):
        pl.semaphore_signal(barrier, inc=1, device_id=(space, summ), device_id_type=MESH)

    greet(me, sibling)
    for step in range(1, YL):
        greet(me, line(step) * CORES + core)
    for step in (1, -1, 2, -2):
        for to_core in range(CORES):
            greet(*ring(step, to_core))

    for step in range(1, X):
        greet(me - x_at + (x_at + step) % X, my_summ)

    @pl.when(me != hub)
    def _():
        greet(hub, my_summ)

    loads = [
        local(codes_in, codes, load_sem.at[0]),
        local(k_weight, weights.at[:, LANES : 2 * LANES], load_sem.at[1]),
        local(v_weight, weights.at[:, 2 * LANES : 3 * LANES], load_sem.at[2]),
        local(q_weight, weights.at[:, 0:LANES], load_sem.at[3]),
        local(picks_in, picks, load_sem.at[4]),
        local(out_weight, out_w, load_sem.at[5]),
        local(gain_in, gain, load_sem.at[6]),
        local(tile_map_in, tile_map, load_sem.at[7]),
        local(pos_bias_in, pos_bias, load_sem.at[8]),
    ]
    half_rows = [pl.ds(half * (TOK // 2), TOK // 2) for half in range(2)]
    own_tokens = [
        local(tokens.at[rows], gathered.at[my_summ, rows], tok_recv.at[half, my_summ])
        for half, rows in enumerate(half_rows)
    ]
    for load in own_tokens:
        load.start()
    for load in loads:
        load.start()
    my_rows = pl.ds(pl.multiple_of(x_at * share, share), share)
    my_cols = pl.ds(pl.multiple_of(my_summ * LANES, LANES), LANES)
    local(sum_keys.at[my_rows, my_cols], keys.at[my_summ], k_recv).start()
    local(sum_values.at[my_rows, my_cols], values.at[my_summ], v_recv).start()

    to_scalars = local(inverse, inverse_s, inverse_sem)

    def prepare():
        loads[7].wait()
        lane = lax.broadcasted_iota(jnp.int32, inverse.shape, 1)

        def place(at, so_far):
            return so_far + jnp.where(lane == tile_map[at], at, 0)

        inverse[...] = lax.fori_loop(0, n_space, place, jnp.zeros(inverse.shape, jnp.int32))
        to_scalars.start()

        loads[0].wait()
        loads[8].wait()

        def fill(at, carry):
            rows = pl.ds(pl.multiple_of(at * UNIT, UNIT), UNIT)
            code = codes[rows, :]
            first = jnp.full(code.shape, HIDDEN, jnp.float32)
            second = first
            for i in range(WIN):
                for j in range(WIN):
                    here = code == i * WIN + j
                    first = jnp.where(here, pos_bias[i, 0, j], first)
                    second = jnp.where(here, pos_bias[i, 1, j], second)
            bias[0, rows, :] = first
            bias[1, rows, :] = second
            return carry

        lax.fori_loop(0, bias.shape[1] // UNIT, fill, 0)
        my_tile = tile_map[me]
        tile_row, tile_col = my_tile // TX, my_tile % TX
        edge = {
            (-1, 0): jnp.where(tile_row > 0, 0.0, HIDDEN),
            (1, 0): jnp.where(tile_row < ty - 1, 0.0, HIDDEN),
            (0, -1): jnp.where(tile_col > 0, 0.0, HIDDEN),
            (0, 1): jnp.where(tile_col < TX - 1, 0.0, HIDDEN),
        }
        for down in (-1, 1):
            for across in (-1, 1):
                edge[down, across] = jnp.minimum(edge[down, 0], edge[0, across])
        for step, hidden in edge.items():
            at = TOK + UNIT_STEP.index(step) * UNIT
            rows = slice(at, at + UNIT_STEP.count(step) * UNIT)
            for h in range(2):
                bias[h, rows, :] = bias[h, rows, :] + hidden

    @pl.when(z_at < LATE_Z)
    def _():
        prepare()

    near = 1 + (YL - 1) + 4 * CORES + (X - 1)
    pl.semaphore_wait(barrier, near + jnp.where(me == hub, n_space - 1, 0))

    @pl.when(me == hub)
    def _():
        def tell(step, carry):
            pl.semaphore_signal(
                entered,
                inc=1,
                device_id=((me + step) % n_space, my_summ),
                device_id_type=MESH,
            )
            return carry

        lax.fori_loop(1, n_space, tell, 0)

    sends = []

    def send_slab(source, slab, half, summ):
        at = gathered.at[slab, half_rows[half]]
        sends.append(
            remote(
                source, at, tok_send.at[len(sends)], tok_recv.at[half, slab], me, summ
            )
        )
        sends[-1].start()

    for half in range(2):
        for step in (2, 1, 3):
            send_slab(tokens.at[half_rows[half]], my_summ, half, line(step) * CORES + core)
        send_slab(tokens.at[half_rows[half]], my_summ, half, sibling)

    def give(source, held, send_sem, recv_sem, space, summ):
        cols = pl.ds(pl.multiple_of(summ * LANES, LANES), LANES)
        remote(source.at[my_rows, cols], held.at[my_summ], send_sem, recv_sem, space, summ).start()

    def give_summary():
        for step in (1, -1):
            for to_core in range(CORES):
                give(sum_keys, keys, k_send, k_recv, *ring(step, to_core))
        for to_core in range(CORES):
            give(sum_keys, keys, k_send, k_recv, *ring(2, to_core))
        give(sum_keys, keys, k_send, k_recv, me, sibling)
        for step in (1, -1):
            for to_core in range(CORES):
                give(sum_values, values, v_send, v_recv, *ring(step, to_core))
        for to_core in range(CORES):
            give(sum_values, values, v_send, v_recv, *ring(-2, to_core))
        give(sum_values, values, v_send, v_recv, me, sibling)

    @pl.when(z_at < LATE_Z)
    def _():
        give_summary()

    def await_slab(slab, half):
        held = gathered.at[slab, half_rows[half]]
        local(held, held, tok_recv.at[half, slab]).wait()

    def await_half(half):
        for step in (1, 3, 2):
            slab = line(step) * CORES + core
            await_slab(slab, half)
            send_slab(gathered.at[slab, half_rows[half]], slab, half, sibling)
        own_tokens[half].wait()
        for step in range(YL):
            await_slab(line(step) * CORES + 1 - core, half)

    def project_half(half):
        rows = half_rows[half]
        squares = jnp.zeros((TOK // 2, LANES), jnp.float32)
        for slab in range(YL * CORES):
            floats = gathered[slab, rows, :].astype(jnp.float32)
            squares = squares + floats * floats
        scale = lax.rsqrt(jnp.sum(squares, axis=-1, keepdims=True) * (1.0 / D) + EPSILON)
        for slab in range(YL * CORES):
            cols = slice(slab * LANES, (slab + 1) * LANES)
            floats = gathered[slab, rows, :].astype(jnp.float32)
            normed[rows, cols] = (floats * scale * gain[:, cols]).astype(jnp.bfloat16)
        result = jnp.dot(normed[rows, :], weights[:, LANES:], preferred_element_type=jnp.float32)
        own_kv[rows, :] = result.astype(jnp.bfloat16)

    bands = BAND // UNIT

    def send_rim(unit, carry):
        router = unit % n_space
        slot = unit // n_space

        @pl.when(router != me)
        def _():
            remote(
                pack.at[unit],
                routed.at[slot, me],
                rim_send,
                rim_recv.at[slot],
                router,
                my_summ,
            ).start()

        @pl.when(router == me)
        def _():
            local(pack.at[unit], routed.at[slot, me], rim_recv.at[slot]).start()

        return carry

    await_half(0)
    loads[6].wait()
    for load in loads[1:3]:
        load.wait()
    project_half(0)

    @pl.when(me != hub)
    def _():
        pl.semaphore_wait(entered, 1)

    for which in range(2):
        cols = slice(which * LANES, (which + 1) * LANES)
        first = which * N_UNIT + bands
        pack[first : first + bands] = own_kv[:BAND, cols].reshape(bands, UNIT, LANES)
        lax.fori_loop(first, first + bands, send_rim, 0)
    await_half(1)
    project_half(1)
    loads[4].wait()
    sides = jnp.dot(
        picks[...].astype(jnp.bfloat16), own_kv[...], preferred_element_type=jnp.float32
    )
    sides = sides.astype(jnp.bfloat16)
    for which in range(2):
        cols = slice(which * LANES, (which + 1) * LANES)
        first = which * N_UNIT
        pack[first : first + bands] = own_kv[TOK - BAND :, cols].reshape(bands, UNIT, LANES)
        pack[first + 2 * bands : first + N_UNIT] = sides[:, cols].reshape(
            N_UNIT - 2 * bands, UNIT, LANES
        )
        lax.fori_loop(first, first + bands, send_rim, 0)
        lax.fori_loop(first + 2 * bands, first + N_UNIT, send_rim, 0)
    own_k = own_kv[:, :LANES]
    own_v = own_kv[:, LANES:]

    loads[3].wait()
    own_q = jnp.dot(normed[...], weights[:, :LANES], preferred_element_type=jnp.float32)
    scaled = own_q.astype(jnp.bfloat16).astype(jnp.float32) * HD ** (-0.5)
    queries[x_at] = scaled.T.astype(jnp.bfloat16)
    peers = [(x_at + step) % X for step in range(X)]
    def one_head(both, h):
        blank = jnp.zeros((HD, TOK), jnp.bfloat16)
        own = both[h * HD : (h + 1) * HD]
        return jnp.concatenate([own, blank] if h == 0 else [blank, own], axis=0)

    def attend(scores, v_rows):
        top = jnp.max(scores, axis=0, keepdims=True)
        weight = jnp.exp(scores - top)
        total = jnp.sum(weight, axis=0, keepdims=True)
        summed = jnp.dot(v_rows, weight.astype(jnp.bfloat16), preferred_element_type=jnp.float32)
        return top, total, summed

    @pl.when(z_at >= LATE_Z)
    def _():
        prepare()

    my_queries = queries[x_at]
    own_vt = own_v.astype(jnp.float32).T.astype(jnp.bfloat16)
    parts = [[], []]
    for h in range(2):
        scores = jnp.dot(own_k, one_head(my_queries, h), preferred_element_type=jnp.float32)
        parts[h].append(attend(scores + bias[h, :TOK], own_vt[h * HD : (h + 1) * HD]))

    for step in range(1, X):
        remote(
            queries.at[x_at],
            queries.at[x_at],
            q_send,
            q_recv.at[x_at],
            me - x_at + peers[step],
            my_summ,
        ).start()

    to_scalars.wait()

    def route():
        for slot in range(slots):
            unit = me + slot * n_space

            @pl.when(unit < 2 * N_UNIT)
            def _():
                local(routed.at[slot], routed.at[slot], rim_recv.at[slot]).wait()
                kind = unit % N_UNIT
                down = jnp.where(
                    kind < 6, -1, jnp.where(kind < 12, 1, jnp.where(kind < 16, 0, jnp.where(kind < 18, -1, 1)))
                )
                across = jnp.where(
                    kind < 12,
                    0,
                    jnp.where(kind < 14, -1, jnp.where(kind < 16, 1, jnp.where(kind % 2 == 0, -1, 1))),
                )

                def pass_on(at, carry):
                    to = at // 8 * 8 + (at + me) % 8
                    tile = tile_map[to]
                    row = jnp.clip(tile // TX + down, 0, ty - 1)
                    col = jnp.clip(tile % TX + across, 0, TX - 1)
                    holder = jnp.clip(inverse_s[0, row * TX + col], 0, n_space - 1)
                    staged[slot, to] = routed[slot, holder]

                    @pl.when(to != me)
                    def _():
                        remote(
                            staged.at[slot, to], halo.at[unit], halo_send, halo_recv, to, my_summ
                        ).start()

                    @pl.when(to == me)
                    def _():
                        local(staged.at[slot, to], halo.at[unit], halo_recv).start()

                    return carry

                lax.fori_loop(0, n_space, pass_on, 0)

    @pl.when(z_at >= LATE_Z)
    def _():
        give_summary()

    before = jnp.where(y_hi == 0, jnp.clip(X - z_at, 0, X), jnp.where(z_at == 0, 2, 0))

    @pl.when(before == 0)
    def _():
        route()

    local(values, values, v_recv).wait()
    for slab in range(YL * CORES):
        values_t[:, slab * share : (slab + 1) * share] = (
            values[slab].astype(jnp.float32).T.astype(jnp.bfloat16)
        )
    local(keys, keys, k_recv).wait()

    def summary(step, carry):
        peer = (x_at + step) % X

        @pl.when(step > 0)
        def _():
            local(queries.at[peer], queries.at[peer], q_recv.at[peer]).wait()

        theirs = queries[peer]
        key_rows = keys[...].reshape(YL * CORES * share, LANES)
        tops, totals, sums = [], [], []
        for h in range(2):
            scores = jnp.dot(key_rows, one_head(theirs, h), preferred_element_type=jnp.float32)
            top, total, summed = attend(scores, values_t[h * HD : (h + 1) * HD, :])
            tops.append(top)
            totals.append(total)
            sums.append(summed)
        part_out[peer] = jnp.concatenate(sums, axis=0).astype(jnp.bfloat16)
        stat_out[peer] = jnp.concatenate(tops + totals + [jnp.zeros((4, TOK), jnp.float32)], axis=0)

        @pl.when(step > 0)
        def _():
            to = me - x_at + peer
            remote(
                part_out.at[peer], part_in.at[x_at], part_send, part_recv.at[x_at], to, my_summ
            ).start()
            remote(
                stat_out.at[peer], stat_in.at[x_at], stat_send, stat_recv.at[x_at], to, my_summ
            ).start()

        return carry

    lax.fori_loop(0, before, summary, 0)

    @pl.when(before > 0)
    def _():
        route()

    lax.fori_loop(before, X, summary, 0)

    local(halo, halo, halo_recv).wait()
    halo_k = halo[:N_UNIT].reshape(HALO_KEYS, LANES)
    halo_vt = halo[N_UNIT:].reshape(HALO_KEYS, LANES).astype(jnp.float32).T.astype(jnp.bfloat16)
    for h in range(2):
        scores = jnp.dot(halo_k, one_head(my_queries, h), preferred_element_type=jnp.float32)
        parts[h].append(attend(scores + bias[h, TOK:], halo_vt[h * HD : (h + 1) * HD]))

    for step in range(X):
        peer = peers[step]
        if step > 0:
            local(part_in.at[peer], part_in.at[peer], part_recv.at[peer]).wait()
            local(stat_in.at[peer], stat_in.at[peer], stat_recv.at[peer]).wait()
            rows, stats = part_in[peer], stat_in[peer]
        else:
            rows, stats = part_out[peer], stat_out[peer]
        for h in range(2):
            parts[h].append(
                (
                    stats[h : h + 1],
                    stats[2 + h : 3 + h],
                    rows[h * HD : (h + 1) * HD].astype(jnp.float32),
                )
            )
    heads = []
    for h in range(2):
        joint = parts[h][0][0]
        for top, _, _ in parts[h][1:]:
            joint = jnp.maximum(joint, top)
        total = jnp.zeros((1, TOK), jnp.float32)
        summed = jnp.zeros((HD, TOK), jnp.float32)
        for top, part_total, part_sum in parts[h]:
            factor = jnp.exp(top - joint)
            total = total + part_total * factor
            summed = summed + part_sum * factor
        heads.append(summed / total)
    attended = jnp.concatenate(heads, axis=0).T.astype(jnp.bfloat16)

    loads[5].wait()
    mixed = jnp.dot(attended, out_w[...], preferred_element_type=jnp.float32).astype(jnp.bfloat16)
    for at in range(YL):
        for side in range(CORES):
            slab = at * CORES + side
            terms[side, at] = mixed[:, slab * LANES : (slab + 1) * LANES]
    rank = jnp.where(y_hi == 0, y_lo, YL - 1 - y_lo)
    others = [at + jnp.where(rank <= at, 1, 0) for at in range(YL - 1)]
    order = [jnp.where(y_hi == 0, other, YL - 1 - other) for other in others] + [y_lo]
    pair = []
    for at in order:
        pair.append(
            remote(
                terms.at[1 - core, at], pair_in.at[at], pair_send.at[at], pair_recv.at[at], me, sibling
            )
        )
        pair[-1].start()
    along = []
    for at in order[:3]:
        local(pair_in.at[at], pair_in.at[at], pair_recv.at[at]).wait()
        both = terms[core, at].astype(jnp.float32) + pair_in[at].astype(jnp.float32)
        pair_sum[at] = both.astype(jnp.bfloat16)
        along.append(
            remote(
                pair_sum.at[at],
                line_in.at[y_lo],
                line_send.at[at],
                line_recv.at[y_lo],
                me,
                at * CORES + core,
            )
        )
        along[-1].start()
    local(pair_in.at[y_lo], pair_in.at[y_lo], pair_recv.at[y_lo]).wait()
    result = terms[core, y_lo].astype(jnp.float32) + pair_in[y_lo].astype(jnp.float32)
    for step in (1, 3, 2):
        at = line(step)
        local(line_in.at[at], line_in.at[at], line_recv.at[at]).wait()
        result = result + line_in[at].astype(jnp.float32)
    out[...] = result.astype(jnp.bfloat16)

    for send in sends + pair + along:
        send.wait_send()
    for sem, held in ((k_send, keys), (v_send, values)):
        sent = held.at[: YL * CORES - 1]
        local(sent, sent, sem).wait()
    for sem, held in ((q_send, queries), (part_send, part_out), (stat_send, stat_out)):
        sent = held.at[: X - 1]
        local(sent, sent, sem).wait()
    routers = [unit % n_space for unit in range(2 * N_UNIT)]
    own_units = jnp.where(me < (2 * N_UNIT) % n_space, 1, 0) + 2 * N_UNIT // n_space
    for count in sorted({routers.count(at) for at in range(n_space)}):

        @pl.when(own_units == count)
        def _():
            sent = pack.at[: 2 * N_UNIT - count]
            local(sent, sent, rim_send).wait()

    for slot in range(slots):

        @pl.when(me + slot * n_space < 2 * N_UNIT)
        def _():
            sent = staged.at[slot, : n_space - 1]
            local(sent, sent, halo_send).wait()


def shards(
    n_space,
    tokens,
    tile_map,
    norm_gain,
    q_weight,
    k_weight,
    v_weight,
    out_weight,
    pos_bias,
    sum_keys,
    sum_values,
):
    share = sum_keys.shape[0] // X
    slots = -(-2 * N_UNIT // n_space)
    bf16 = jnp.bfloat16
    f32 = jnp.float32
    dma = pltpu.SemaphoreType.DMA
    anywhere = pl.BlockSpec(memory_space=pl.ANY)
    vector = pl.BlockSpec(memory_space=pltpu.VMEM)
    slab = (TOK, LANES)
    turned = (LANES, TOK)
    scratch = [
        pltpu.SMEM((n_space,), jnp.int32),
        pltpu.SMEM((WIN, 2, WIN), f32),
        pltpu.VMEM((1, D), f32),
        pltpu.VMEM((YL * CORES,) + slab, bf16),
        pltpu.VMEM((TOK, D), bf16),
        pltpu.VMEM((D, 3 * LANES), bf16),
        pltpu.VMEM((LANES, D), bf16),
        pltpu.VMEM((TOK + HALO_KEYS, TOK), jnp.int32),
        pltpu.VMEM((SIDE_ROWS, TOK), f32),
        pltpu.VMEM((2, TOK + HALO_KEYS, TOK), f32),
        pltpu.VMEM((TOK, 2 * LANES), bf16),
        pltpu.VMEM((YL * CORES, share, LANES), bf16),
        pltpu.VMEM((YL * CORES, share, LANES), bf16),
        pltpu.VMEM((LANES, YL * CORES * share), bf16),
        pltpu.VMEM((X,) + turned, bf16),
        pltpu.VMEM((X,) + turned, bf16),
        pltpu.VMEM((X,) + turned, bf16),
        pltpu.VMEM((X, 8, TOK), f32),
        pltpu.VMEM((X, 8, TOK), f32),
        pltpu.VMEM((8, LANES), jnp.int32),
        pltpu.SMEM((8, LANES), jnp.int32),
        pltpu.VMEM((2 * N_UNIT, UNIT, LANES), bf16),
        pltpu.VMEM((slots, n_space, UNIT, LANES), bf16),
        pltpu.VMEM((slots, n_space, UNIT, LANES), bf16),
        pltpu.VMEM((2 * N_UNIT, UNIT, LANES), bf16),
        pltpu.VMEM((CORES, YL) + slab, bf16),
        pltpu.VMEM((YL,) + slab, bf16),
        pltpu.VMEM((YL,) + slab, bf16),
        pltpu.VMEM((YL,) + slab, bf16),
        dma((9,)),
        dma,
        pltpu.SemaphoreType.REGULAR,
        dma((14,)),
        dma((2, YL * CORES)),
        dma,
        dma,
        dma,
        dma,
        dma,
        dma((X,)),
        dma,
        dma((X,)),
        dma,
        dma((X,)),
        dma,
        dma((slots,)),
        dma,
        dma,
        dma((YL,)),
        dma((YL,)),
        dma((YL,)),
        dma((YL,)),
    ]
    mixed = pl.pallas_call(
        partial(kernel, n_space),
        out_shape=jax.ShapeDtypeStruct(slab, bf16),
        in_specs=[anywhere] * 12,
        out_specs=vector,
        scratch_shapes=scratch,
        compiler_params=pltpu.CompilerParams(
            collective_id=0, has_side_effects=True, vmem_limit_bytes=63 * 1024 * 1024
        ),
        name="tile_attention",
    )(
        tile_map,
        pos_bias.transpose(1, 0, 2),
        tokens.reshape(slab),
        norm_gain.reshape(1, D),
        q_weight,
        k_weight,
        v_weight,
        out_weight,
        sum_keys,
        sum_values,
        jnp.asarray(offset_codes()),
        jnp.asarray(side_picks()),
    )
    return mixed.reshape(1, BH, BW, LANES)


def solution(mesh):
    return jax.shard_map(
        partial(shards, mesh.shape["space"]),
        mesh=mesh,
        in_specs=(
            P("space", None, None, "summ"),
            P(),
            P(),
            P(None, "summ"),
            P(None, "summ"),
            P(None, "summ"),
            P("summ", None),
            P("summ", None, None),
            P("summ", None),
            P("summ", None),
        ),
        out_specs=P("space", None, None, "summ"),
        check_vma=False,
    )
```

```python
from functools import partial

import numpy as np
import jax
import jax.numpy as jnp
from jax import lax
from jax.experimental import pallas as pl
from jax.experimental.pallas import tpu as pltpu
from jax.sharding import PartitionSpec as P

D = 1024
HD = 64
HALO = 3
TX = 8
BW = 32
BH = 8
EPSILON = 1e-05
WIN = 2 * HALO + 1
TOK = BH * BW
LANES = 128
X = 4
YH = 2
YL = 4
CORES = 2
HIDDEN = -1e30
UNIT = 16
UNIT_STEP = (
    [(-1, 0)] * 6
    + [(1, 0)] * 6
    + [(0, -1)] * 2
    + [(0, 1)] * 2
    + [(-1, -1), (-1, 1), (1, -1), (1, 1)]
)
N_UNIT = len(UNIT_STEP)
HALO_KEYS = N_UNIT * UNIT
BAND = HALO * BW
SIDE_ROWS = HALO_KEYS - 2 * BAND
LATE_Z = 5
MESH = pl.DeviceIdType.MESH


def halo_positions():
    places = [(-HALO + j // BW, j % BW, (BH - HALO) * BW + j) for j in range(BAND)]
    places += [(BH + j // BW, j % BW, j) for j in range(BAND)]

    def side(count, rows, padded, row_at, col_at, from_row, from_col):
        out = []
        for i in range(padded):
            r, c = i // HALO, i % HALO
            out.append((row_at + r, col_at + c, (from_row + r) * BW + from_col + c) if i < count else None)
        return out

    places += side(BH * HALO, BH, 2 * UNIT, 0, -HALO, 0, BW - HALO)
    places += side(BH * HALO, BH, 2 * UNIT, 0, BW, 0, 0)
    places += side(HALO * HALO, HALO, UNIT, -HALO, -HALO, BH - HALO, BW - HALO)
    places += side(HALO * HALO, HALO, UNIT, -HALO, BW, BH - HALO, 0)
    places += side(HALO * HALO, HALO, UNIT, BH, -HALO, 0, BW - HALO)
    places += side(HALO * HALO, HALO, UNIT, BH, BW, 0, 0)
    return places


def offset_codes():
    keys = [(k // BW, k % BW) for k in range(TOK)]
    keys += [(None if place is None else place[:2]) for place in halo_positions()]
    codes = np.full((len(keys), TOK), -1, np.int32)
    rows, cols = np.arange(TOK) // BW, np.arange(TOK) % BW
    for at, key in enumerate(keys):
        if key is None:
            continue
        i, j = key[0] - rows + HALO, key[1] - cols + HALO
        near = (i >= 0) & (i < WIN) & (j >= 0) & (j < WIN)
        codes[at] = np.where(near, i * WIN + j, -1)
    return codes


def side_picks():
    picks = np.zeros((SIDE_ROWS, TOK), np.float32)
    for at, place in enumerate(halo_positions()[2 * BAND :]):
        if place is not None:
            picks[at, place[2]] = 1.0
    return picks


def kernel(
    n_space,
    tile_map_in,
    pos_bias_in,
    tokens,
    gain_in,
    q_weight,
    k_weight,
    v_weight,
    out_weight,
    sum_keys,
    sum_values,
    codes_in,
    picks_in,
    out,
    tile_map,
    pos_bias,
    gain,
    gathered,
    normed,
    weights,
    out_w,
    codes,
    picks,
    bias,
    own_kv,
    keys,
    values,
    values_t,
    queries,
    part_out,
    part_in,
    stat_out,
    stat_in,
    inverse,
    inverse_s,
    pack,
    routed,
    staged,
    halo,
    attended,
    terms,
    line_in,
    load_sem,
    inverse_sem,
    entered,
    tok_send,
    tok_recv,
    k_send,
    k_recv,
    v_send,
    v_recv,
    q_send,
    q_recv,
    part_send,
    part_recv,
    stat_send,
    stat_recv,
    rim_send,
    rim_recv,
    halo_send,
    halo_recv,
    weight_send,
    weight_recv,
    attended_send,
    attended_recv,
    line_send,
    line_recv,
):
    slots = routed.shape[0]
    hub = n_space - 1
    share = keys.shape[1]
    ty = n_space // TX
    me = lax.axis_index("space")
    my_summ = lax.axis_index("summ")
    y_lo, core = my_summ // CORES, my_summ % CORES
    x_at = me % X
    y_hi = (me // X) % YH
    z_at = me // (X * YH)
    y_at = y_hi * YL + y_lo
    sibling = y_lo * CORES + 1 - core

    def local(src, dst, sem):
        return pltpu.make_async_copy(src, dst, sem)

    def remote(src, dst, send, recv, space, summ):
        return pltpu.make_async_remote_copy(
            src_ref=src,
            dst_ref=dst,
            send_sem=send,
            recv_sem=recv,
            device_id=(space, summ),
            device_id_type=MESH,
        )

    def ring(step, to_core):
        y = (y_at + step + YH * YL) % (YH * YL)
        return (z_at * YH + y // YL) * X + x_at, (y % YL) * CORES + to_core

    def line(step):
        return (y_lo + step) % YL

    barrier = pltpu.get_barrier_semaphore()

    def greet(space, summ):
        pl.semaphore_signal(barrier, inc=1, device_id=(space, summ), device_id_type=MESH)

    greet(me, sibling)
    for step in range(1, YL):
        greet(me, line(step) * CORES + core)
    for step in (1, -1, 2, -2):
        for to_core in range(CORES):
            greet(*ring(step, to_core))

    for step in range(1, X):
        greet(me - x_at + (x_at + step) % X, my_summ)

    @pl.when(me != hub)
    def _():
        greet(hub, my_summ)

    loads = [
        local(codes_in, codes, load_sem.at[0]),
        local(k_weight, weights.at[:, LANES : 2 * LANES], load_sem.at[1]),
        local(v_weight, weights.at[:, 2 * LANES : 3 * LANES], load_sem.at[2]),
        local(q_weight, weights.at[:, 0:LANES], load_sem.at[3]),
        local(picks_in, picks, load_sem.at[4]),
        local(gain_in, gain, load_sem.at[5]),
        local(tile_map_in, tile_map, load_sem.at[6]),
        local(pos_bias_in, pos_bias, load_sem.at[7]),
    ]
    half_rows = [pl.ds(half * (TOK // 2), TOK // 2) for half in range(2)]
    own_tokens = [
        local(tokens.at[rows], gathered.at[my_summ, rows], tok_recv.at[half, my_summ])
        for half, rows in enumerate(half_rows)
    ]
    for load in own_tokens:
        load.start()
    for load in loads:
        load.start()

    def out_cols(at, side):
        return pl.ds(pl.multiple_of((at * CORES + side) * LANES, LANES), LANES)

    for at in range(YL):
        cols = slice(at * LANES, (at + 1) * LANES)
        local(out_weight.at[:, out_cols(at, core)], out_w.at[:LANES, cols], load_sem.at[8]).start()
    my_rows = pl.ds(pl.multiple_of(x_at * share, share), share)
    my_cols = pl.ds(pl.multiple_of(my_summ * LANES, LANES), LANES)
    local(sum_keys.at[my_rows, my_cols], keys.at[my_summ], k_recv).start()
    local(sum_values.at[my_rows, my_cols], values.at[my_summ], v_recv).start()

    to_scalars = local(inverse, inverse_s, inverse_sem)

    def prepare():
        loads[6].wait()
        lane = lax.broadcasted_iota(jnp.int32, inverse.shape, 1)

        def place(at, so_far):
            return so_far + jnp.where(lane == tile_map[at], at, 0)

        inverse[...] = lax.fori_loop(0, n_space, place, jnp.zeros(inverse.shape, jnp.int32))
        to_scalars.start()

        loads[0].wait()
        loads[7].wait()

        def fill(at, carry):
            rows = pl.ds(pl.multiple_of(at * UNIT, UNIT), UNIT)
            code = codes[rows, :]
            first = jnp.full(code.shape, HIDDEN, jnp.float32)
            second = first
            for i in range(WIN):
                for j in range(WIN):
                    here = code == i * WIN + j
                    first = jnp.where(here, pos_bias[i, 0, j], first)
                    second = jnp.where(here, pos_bias[i, 1, j], second)
            bias[0, rows, :] = first
            bias[1, rows, :] = second
            return carry

        lax.fori_loop(0, bias.shape[1] // UNIT, fill, 0)
        my_tile = tile_map[me]
        tile_row, tile_col = my_tile // TX, my_tile % TX
        edge = {
            (-1, 0): jnp.where(tile_row > 0, 0.0, HIDDEN),
            (1, 0): jnp.where(tile_row < ty - 1, 0.0, HIDDEN),
            (0, -1): jnp.where(tile_col > 0, 0.0, HIDDEN),
            (0, 1): jnp.where(tile_col < TX - 1, 0.0, HIDDEN),
        }
        for down in (-1, 1):
            for across in (-1, 1):
                edge[down, across] = jnp.minimum(edge[down, 0], edge[0, across])
        for step, hidden in edge.items():
            at = TOK + UNIT_STEP.index(step) * UNIT
            rows = slice(at, at + UNIT_STEP.count(step) * UNIT)
            for h in range(2):
                bias[h, rows, :] = bias[h, rows, :] + hidden

    @pl.when(z_at < LATE_Z)
    def _():
        prepare()

    near = 1 + (YL - 1) + 4 * CORES + (X - 1)
    pl.semaphore_wait(barrier, near + jnp.where(me == hub, n_space - 1, 0))

    @pl.when(me == hub)
    def _():
        def tell(step, carry):
            pl.semaphore_signal(
                entered,
                inc=1,
                device_id=((me + step) % n_space, my_summ),
                device_id_type=MESH,
            )
            return carry

        lax.fori_loop(1, n_space, tell, 0)

    sends = []

    def send_slab(source, slab, half, summ):
        at = gathered.at[slab, half_rows[half]]
        sends.append(
            remote(
                source, at, tok_send.at[len(sends)], tok_recv.at[half, slab], me, summ
            )
        )
        sends[-1].start()

    for half in range(2):
        for step in (2, 1, 3):
            send_slab(tokens.at[half_rows[half]], my_summ, half, line(step) * CORES + core)
        send_slab(tokens.at[half_rows[half]], my_summ, half, sibling)

    for at in range(YL):
        cols = slice(at * LANES, (at + 1) * LANES)
        remote(
            out_weight.at[:, out_cols(at, 1 - core)],
            out_w.at[LANES:, cols],
            weight_send,
            weight_recv,
            me,
            sibling,
        ).start()

    def give(source, held, send_sem, recv_sem, space, summ):
        cols = pl.ds(pl.multiple_of(summ * LANES, LANES), LANES)
        remote(source.at[my_rows, cols], held.at[my_summ], send_sem, recv_sem, space, summ).start()

    def give_summary():
        for step in (1, -1):
            for to_core in range(CORES):
                give(sum_keys, keys, k_send, k_recv, *ring(step, to_core))
        for to_core in range(CORES):
            give(sum_keys, keys, k_send, k_recv, *ring(2, to_core))
        give(sum_keys, keys, k_send, k_recv, me, sibling)
        for step in (1, -1):
            for to_core in range(CORES):
                give(sum_values, values, v_send, v_recv, *ring(step, to_core))
        for to_core in range(CORES):
            give(sum_values, values, v_send, v_recv, *ring(-2, to_core))
        give(sum_values, values, v_send, v_recv, me, sibling)

    @pl.when(z_at < LATE_Z)
    def _():
        give_summary()

    def await_slab(slab, half):
        held = gathered.at[slab, half_rows[half]]
        local(held, held, tok_recv.at[half, slab]).wait()

    def await_half(half):
        for step in (1, 3, 2):
            slab = line(step) * CORES + core
            await_slab(slab, half)
            send_slab(gathered.at[slab, half_rows[half]], slab, half, sibling)
        own_tokens[half].wait()
        for step in range(YL):
            await_slab(line(step) * CORES + 1 - core, half)

    def project_half(half):
        rows = half_rows[half]
        squares = jnp.zeros((TOK // 2, LANES), jnp.float32)
        for slab in range(YL * CORES):
            floats = gathered[slab, rows, :].astype(jnp.float32)
            squares = squares + floats * floats
        scale = lax.rsqrt(jnp.sum(squares, axis=-1, keepdims=True) * (1.0 / D) + EPSILON)
        for slab in range(YL * CORES):
            cols = slice(slab * LANES, (slab + 1) * LANES)
            floats = gathered[slab, rows, :].astype(jnp.float32)
            normed[rows, cols] = (floats * scale * gain[:, cols]).astype(jnp.bfloat16)
        result = jnp.dot(normed[rows, :], weights[:, LANES:], preferred_element_type=jnp.float32)
        own_kv[rows, :] = result.astype(jnp.bfloat16)

    bands = BAND // UNIT

    def send_rim(unit, carry):
        router = unit % n_space
        slot = unit // n_space

        @pl.when(router != me)
        def _():
            remote(
                pack.at[unit],
                routed.at[slot, me],
                rim_send,
                rim_recv.at[slot],
                router,
                my_summ,
            ).start()

        @pl.when(router == me)
        def _():
            local(pack.at[unit], routed.at[slot, me], rim_recv.at[slot]).start()

        return carry

    await_half(0)
    loads[5].wait()
    for load in loads[1:3]:
        load.wait()
    project_half(0)

    @pl.when(me != hub)
    def _():
        pl.semaphore_wait(entered, 1)

    for which in range(2):
        cols = slice(which * LANES, (which + 1) * LANES)
        first = which * N_UNIT + bands
        pack[first : first + bands] = own_kv[:BAND, cols].reshape(bands, UNIT, LANES)
        lax.fori_loop(first, first + bands, send_rim, 0)
    await_half(1)
    project_half(1)
    loads[4].wait()
    sides = jnp.dot(
        picks[...].astype(jnp.bfloat16), own_kv[...], preferred_element_type=jnp.float32
    )
    sides = sides.astype(jnp.bfloat16)
    for which in range(2):
        cols = slice(which * LANES, (which + 1) * LANES)
        first = which * N_UNIT
        pack[first : first + bands] = own_kv[TOK - BAND :, cols].reshape(bands, UNIT, LANES)
        pack[first + 2 * bands : first + N_UNIT] = sides[:, cols].reshape(
            N_UNIT - 2 * bands, UNIT, LANES
        )
        lax.fori_loop(first, first + bands, send_rim, 0)
        lax.fori_loop(first + 2 * bands, first + N_UNIT, send_rim, 0)
    own_k = own_kv[:, :LANES]
    own_v = own_kv[:, LANES:]

    loads[3].wait()
    own_q = jnp.dot(normed[...], weights[:, :LANES], preferred_element_type=jnp.float32)
    scaled = own_q.astype(jnp.bfloat16).astype(jnp.float32) * HD ** (-0.5)
    queries[x_at] = scaled.T.astype(jnp.bfloat16)
    peers = [(x_at + step) % X for step in range(X)]
    def one_head(both, h):
        blank = jnp.zeros((HD, TOK), jnp.bfloat16)
        own = both[h * HD : (h + 1) * HD]
        return jnp.concatenate([own, blank] if h == 0 else [blank, own], axis=0)

    def attend(scores, v_rows):
        top = jnp.max(scores, axis=0, keepdims=True)
        weight = jnp.exp(scores - top)
        total = jnp.sum(weight, axis=0, keepdims=True)
        summed = jnp.dot(v_rows, weight.astype(jnp.bfloat16), preferred_element_type=jnp.float32)
        return top, total, summed

    @pl.when(z_at >= LATE_Z)
    def _():
        prepare()

    my_queries = queries[x_at]
    own_vt = own_v.astype(jnp.float32).T.astype(jnp.bfloat16)
    parts = [[], []]
    for h in range(2):
        scores = jnp.dot(own_k, one_head(my_queries, h), preferred_element_type=jnp.float32)
        parts[h].append(attend(scores + bias[h, :TOK], own_vt[h * HD : (h + 1) * HD]))

    for step in range(1, X):
        remote(
            queries.at[x_at],
            queries.at[x_at],
            q_send,
            q_recv.at[x_at],
            me - x_at + peers[step],
            my_summ,
        ).start()

    to_scalars.wait()

    def route():
        for slot in range(slots):
            unit = me + slot * n_space

            @pl.when(unit < 2 * N_UNIT)
            def _():
                local(routed.at[slot], routed.at[slot], rim_recv.at[slot]).wait()
                kind = unit % N_UNIT
                down = jnp.where(
                    kind < 6, -1, jnp.where(kind < 12, 1, jnp.where(kind < 16, 0, jnp.where(kind < 18, -1, 1)))
                )
                across = jnp.where(
                    kind < 12,
                    0,
                    jnp.where(kind < 14, -1, jnp.where(kind < 16, 1, jnp.where(kind % 2 == 0, -1, 1))),
                )

                def pass_on(at, carry):
                    to = at // 8 * 8 + (at + me) % 8
                    tile = tile_map[to]
                    row = jnp.clip(tile // TX + down, 0, ty - 1)
                    col = jnp.clip(tile % TX + across, 0, TX - 1)
                    holder = jnp.clip(inverse_s[0, row * TX + col], 0, n_space - 1)
                    staged[slot, to] = routed[slot, holder]

                    @pl.when(to != me)
                    def _():
                        remote(
                            staged.at[slot, to], halo.at[unit], halo_send, halo_recv, to, my_summ
                        ).start()

                    @pl.when(to == me)
                    def _():
                        local(staged.at[slot, to], halo.at[unit], halo_recv).start()

                    return carry

                lax.fori_loop(0, n_space, pass_on, 0)

    @pl.when(z_at >= LATE_Z)
    def _():
        give_summary()

    before = jnp.where(y_hi == 0, jnp.clip(X - z_at, 0, X), jnp.where(z_at == 0, 2, 0))

    @pl.when(before == 0)
    def _():
        route()

    local(values, values, v_recv).wait()
    for slab in range(YL * CORES):
        values_t[:, slab * share : (slab + 1) * share] = (
            values[slab].astype(jnp.float32).T.astype(jnp.bfloat16)
        )
    local(keys, keys, k_recv).wait()

    def summary(step, carry):
        peer = (x_at + step) % X

        @pl.when(step > 0)
        def _():
            local(queries.at[peer], queries.at[peer], q_recv.at[peer]).wait()

        theirs = queries[peer]
        key_rows = keys[...].reshape(YL * CORES * share, LANES)
        tops, totals, sums = [], [], []
        for h in range(2):
            scores = jnp.dot(key_rows, one_head(theirs, h), preferred_element_type=jnp.float32)
            top, total, summed = attend(scores, values_t[h * HD : (h + 1) * HD, :])
            tops.append(top)
            totals.append(total)
            sums.append(summed)
        part_out[peer] = jnp.concatenate(sums, axis=0).astype(jnp.bfloat16)
        stat_out[peer] = jnp.concatenate(tops + totals + [jnp.zeros((4, TOK), jnp.float32)], axis=0)

        @pl.when(step > 0)
        def _():
            to = me - x_at + peer
            remote(
                part_out.at[peer], part_in.at[x_at], part_send, part_recv.at[x_at], to, my_summ
            ).start()
            remote(
                stat_out.at[peer], stat_in.at[x_at], stat_send, stat_recv.at[x_at], to, my_summ
            ).start()

        return carry

    lax.fori_loop(0, before, summary, 0)

    @pl.when(before > 0)
    def _():
        route()

    lax.fori_loop(before, X, summary, 0)

    local(halo, halo, halo_recv).wait()
    halo_k = halo[:N_UNIT].reshape(HALO_KEYS, LANES)
    halo_vt = halo[N_UNIT:].reshape(HALO_KEYS, LANES).astype(jnp.float32).T.astype(jnp.bfloat16)
    for h in range(2):
        scores = jnp.dot(halo_k, one_head(my_queries, h), preferred_element_type=jnp.float32)
        parts[h].append(attend(scores + bias[h, TOK:], halo_vt[h * HD : (h + 1) * HD]))

    for step in range(X):
        peer = peers[step]
        if step > 0:
            local(part_in.at[peer], part_in.at[peer], part_recv.at[peer]).wait()
            local(stat_in.at[peer], stat_in.at[peer], stat_recv.at[peer]).wait()
            rows, stats = part_in[peer], stat_in[peer]
        else:
            rows, stats = part_out[peer], stat_out[peer]
        for h in range(2):
            parts[h].append(
                (
                    stats[h : h + 1],
                    stats[2 + h : 3 + h],
                    rows[h * HD : (h + 1) * HD].astype(jnp.float32),
                )
            )
    heads = []
    for h in range(2):
        joint = parts[h][0][0]
        for top, _, _ in parts[h][1:]:
            joint = jnp.maximum(joint, top)
        total = jnp.zeros((1, TOK), jnp.float32)
        summed = jnp.zeros((HD, TOK), jnp.float32)
        for top, part_total, part_sum in parts[h]:
            factor = jnp.exp(top - joint)
            total = total + part_total * factor
            summed = summed + part_sum * factor
        heads.append(summed / total)
    attended[0] = jnp.concatenate(heads, axis=0).T.astype(jnp.bfloat16)

    share_heads = remote(
        attended.at[0], attended.at[1], attended_send, attended_recv, me, sibling
    )
    share_heads.start()
    local(out_w.at[:LANES], out_w.at[:LANES], load_sem.at[8]).wait()
    local(out_w.at[LANES:], out_w.at[LANES:], weight_recv).wait()
    mixed = jnp.dot(attended[0], out_w[:LANES, :], preferred_element_type=jnp.float32)
    local(attended.at[1], attended.at[1], attended_recv).wait()
    mixed = mixed + jnp.dot(attended[1], out_w[LANES:, :], preferred_element_type=jnp.float32)
    for at in range(YL):
        terms[at] = mixed[:, at * LANES : (at + 1) * LANES].astype(jnp.bfloat16)
    along = []
    rank = jnp.where(y_hi == 0, y_lo, YL - 1 - y_lo)
    for other in range(YL - 1):
        other = other + jnp.where(rank <= other, 1, 0)
        at = jnp.where(y_hi == 0, other, YL - 1 - other)
        along.append(
            remote(
                terms.at[at],
                line_in.at[y_lo],
                line_send.at[at],
                line_recv.at[y_lo],
                me,
                at * CORES + core,
            )
        )
        along[-1].start()
    result = terms[y_lo].astype(jnp.float32)
    for step in (1, 3, 2):
        at = line(step)
        local(line_in.at[at], line_in.at[at], line_recv.at[at]).wait()
        result = result + line_in[at].astype(jnp.float32)
    out[...] = result.astype(jnp.bfloat16)

    for send in sends + [share_heads] + along:
        send.wait_send()
    local(out_w.at[LANES:], out_w.at[LANES:], weight_send).wait()
    for sem, held in ((k_send, keys), (v_send, values)):
        sent = held.at[: YL * CORES - 1]
        local(sent, sent, sem).wait()
    for sem, held in ((q_send, queries), (part_send, part_out), (stat_send, stat_out)):
        sent = held.at[: X - 1]
        local(sent, sent, sem).wait()
    routers = [unit % n_space for unit in range(2 * N_UNIT)]
    own_units = jnp.where(me < (2 * N_UNIT) % n_space, 1, 0) + 2 * N_UNIT // n_space
    for count in sorted({routers.count(at) for at in range(n_space)}):

        @pl.when(own_units == count)
        def _():
            sent = pack.at[: 2 * N_UNIT - count]
            local(sent, sent, rim_send).wait()

    for slot in range(slots):

        @pl.when(me + slot * n_space < 2 * N_UNIT)
        def _():
            sent = staged.at[slot, : n_space - 1]
            local(sent, sent, halo_send).wait()


def shards(
    n_space,
    tokens,
    tile_map,
    norm_gain,
    q_weight,
    k_weight,
    v_weight,
    out_weight,
    pos_bias,
    sum_keys,
    sum_values,
):
    share = sum_keys.shape[0] // X
    slots = -(-2 * N_UNIT // n_space)
    bf16 = jnp.bfloat16
    f32 = jnp.float32
    dma = pltpu.SemaphoreType.DMA
    anywhere = pl.BlockSpec(memory_space=pl.ANY)
    vector = pl.BlockSpec(memory_space=pltpu.VMEM)
    slab = (TOK, LANES)
    turned = (LANES, TOK)
    scratch = [
        pltpu.SMEM((n_space,), jnp.int32),
        pltpu.SMEM((WIN, 2, WIN), f32),
        pltpu.VMEM((1, D), f32),
        pltpu.VMEM((YL * CORES,) + slab, bf16),
        pltpu.VMEM((TOK, D), bf16),
        pltpu.VMEM((D, 3 * LANES), bf16),
        pltpu.VMEM((CORES * LANES, YL * LANES), bf16),
        pltpu.VMEM((TOK + HALO_KEYS, TOK), jnp.int32),
        pltpu.VMEM((SIDE_ROWS, TOK), f32),
        pltpu.VMEM((2, TOK + HALO_KEYS, TOK), f32),
        pltpu.VMEM((TOK, 2 * LANES), bf16),
        pltpu.VMEM((YL * CORES, share, LANES), bf16),
        pltpu.VMEM((YL * CORES, share, LANES), bf16),
        pltpu.VMEM((LANES, YL * CORES * share), bf16),
        pltpu.VMEM((X,) + turned, bf16),
        pltpu.VMEM((X,) + turned, bf16),
        pltpu.VMEM((X,) + turned, bf16),
        pltpu.VMEM((X, 8, TOK), f32),
        pltpu.VMEM((X, 8, TOK), f32),
        pltpu.VMEM((8, LANES), jnp.int32),
        pltpu.SMEM((8, LANES), jnp.int32),
        pltpu.VMEM((2 * N_UNIT, UNIT, LANES), bf16),
        pltpu.VMEM((slots, n_space, UNIT, LANES), bf16),
        pltpu.VMEM((slots, n_space, UNIT, LANES), bf16),
        pltpu.VMEM((2 * N_UNIT, UNIT, LANES), bf16),
        pltpu.VMEM((CORES,) + slab, bf16),
        pltpu.VMEM((YL,) + slab, bf16),
        pltpu.VMEM((YL,) + slab, bf16),
        dma((9,)),
        dma,
        pltpu.SemaphoreType.REGULAR,
        dma((14,)),
        dma((2, YL * CORES)),
        dma,
        dma,
        dma,
        dma,
        dma,
        dma((X,)),
        dma,
        dma((X,)),
        dma,
        dma((X,)),
        dma,
        dma((slots,)),
        dma,
        dma,
        dma,
        dma,
        dma,
        dma,
        dma((YL,)),
        dma((YL,)),
    ]
    mixed = pl.pallas_call(
        partial(kernel, n_space),
        out_shape=jax.ShapeDtypeStruct(slab, bf16),
        in_specs=[anywhere] * 12,
        out_specs=vector,
        scratch_shapes=scratch,
        compiler_params=pltpu.CompilerParams(
            collective_id=0, has_side_effects=True, vmem_limit_bytes=63 * 1024 * 1024
        ),
        name="tile_attention",
    )(
        tile_map,
        pos_bias.transpose(1, 0, 2),
        tokens.reshape(slab),
        norm_gain.reshape(1, D),
        q_weight,
        k_weight,
        v_weight,
        out_weight,
        sum_keys,
        sum_values,
        jnp.asarray(offset_codes()),
        jnp.asarray(side_picks()),
    )
    return mixed.reshape(1, BH, BW, LANES)


def solution(mesh):
    return jax.shard_map(
        partial(shards, mesh.shape["space"]),
        mesh=mesh,
        in_specs=(
            P("space", None, None, "summ"),
            P(),
            P(),
            P(None, "summ"),
            P(None, "summ"),
            P(None, "summ"),
            P("summ", None),
            P("summ", None, None),
            P("summ", None),
            P("summ", None),
        ),
        out_specs=P("space", None, None, "summ"),
        check_vma=False,
    )
```
